128 devices in a mesh: node: 16 (over x_hi, y, core), local: 8 (over z, x_lo).
Axes of the slice: x: 4 (x_hi: 2, x_lo: 2; x = x_hi * 2 + x_lo), y: 4, z: 4, core: 2. Of those that a mesh axis runs over, the one named last changes fastest.
Arguments:
- query: bfloat16 [4096, 16384], P(None, ('node', 'local')), may hold values from -6 to 6
- key_in: bfloat16 [4096, 16384], P(None, ('node', 'local')), may hold values from -6 to 6
- value_in: bfloat16 [4096, 16384], P(None, ('node', 'local')), may hold values from -6 to 6
- filters: float32 [4096, 16384], P(('node', 'local')), may hold values from -2 to 2
- skip_gain: float32 [4096], replicated, may hold values from -4 to 4
- cotangent: bfloat16 [4096, 16384], P(None, ('node', 'local')), may hold values from -6 to 6
Outputs:
- output: bfloat16 [4096, 16384], P(None, ('node', 'local'))
- grad_query: bfloat16 [4096, 16384], P(None, ('node', 'local'))
- grad_key: bfloat16 [4096, 16384], P(None, ('node', 'local'))
- grad_value: bfloat16 [4096, 16384], P(None, ('node', 'local'))
- grad_filters: float32 [4096, 16384], P(('node', 'local'))
- grad_skip: float32 [4096], P(('node', 'local'))
The draws below stay inside these ranges and needn't reach their ends.
All inputs are finite; a program needn't handle non-finite values.
Results may differ from the reference program's by a relative error of at most 0.0053.
Values may be sent and summed in bfloat16 or wider, within the bound.
No kernel may reach another device: no remote copies, remote signals or barrier semaphores. Data moves between devices by JAX's collectives and lax.ppermute only.
A program may use at most 192 MiB of HBM per device.

```python
import jax
import jax.numpy as jnp
from jax import lax

C = 4096
SEQ = 16384


def draw_filters(key, part):
    key = jax.random.fold_in(key, 7)
    key_rate, key_pick, key_noise = jax.random.split(key, 3)
    seq_len = jnp.float32(SEQ)
    spread = jax.random.uniform(key_rate, (C, 1), jnp.float32)
    slow_rate = jnp.exp(jnp.log(0.1 / seq_len) + spread * jnp.log(20.0))
    fast_rate = jnp.exp(jnp.log(2.0 / seq_len) + spread * (jnp.log(1.0 / 30.0) - jnp.log(2.0 / seq_len)))
    picked = jax.random.uniform(key_pick, (C, 1), jnp.float32) < 0.5
    rate = jnp.where(picked, slow_rate, fast_rate)
    noise = jax.random.truncated_normal(key_noise, -4.0, 4.0, (C, SEQ), jnp.float32)
    steps = jnp.arange(SEQ, dtype=jnp.float32)[None, :]
    norm_scale = jnp.sqrt((1.0 - jnp.exp(-2.0 * rate)) / (1.0 - jnp.exp(-2.0 * rate * seq_len)))
    return (noise * jnp.exp(-rate * steps) * norm_scale).astype(jnp.float32)


def shard_levels(rng, dims, shards, least, top_value):
    level = 1.0
    for position, blocks in shards:
        draws = jax.random.uniform(jax.random.fold_in(jax.random.fold_in(rng, 6), position), (blocks,), jnp.float32, least / len(shards), top_value / len(shards))
        level = level * jnp.repeat(jnp.exp(draws), dims[position] // blocks).reshape((-1,) + (1,) * (len(dims) - 1 - position))
    return level


def scatter_about(stream_key, dims, width, bound, shards=(), kind=jnp.bfloat16):
    entries = jax.random.normal(stream_key, dims, jnp.float32) * width
    if len(shards) > 0:
        entries = shard_levels(stream_key, dims, shards, -0.22, 0.18) * entries
    return jnp.clip(entries, min=-bound, max=bound).astype(kind)


def setup_inputs(seed: int = 0) -> dict:
    seeds = jax.random.split(jax.random.key(seed), 7)
    return {
        "query": scatter_about(seeds[0], (C, SEQ), 1.0, 6.0, ((1, 128),)),
        "key_in": scatter_about(seeds[1], (C, SEQ), 1.0, 6.0, ((1, 128),)),
        "value_in": scatter_about(seeds[2], (C, SEQ), 1.0, 6.0, ((1, 128),)),
        "filters": draw_filters(jax.random.fold_in(seeds[6], 71), 0),
        "skip_gain": scatter_about(seeds[4], (C,), 1.0, 4.0, (), jnp.float32),
        "cotangent": scatter_about(seeds[5], (C, SEQ), 1.0, 6.0, ((1, 128),)),
    }


def block_spectra(block):
    filt, mix, wgt = block
    full = 2 * SEQ
    spec_fil = jnp.fft.rfft(filt, n=full, axis=-1)
    spec_mix = jnp.fft.rfft(mix.astype(jnp.float32), n=full, axis=-1)
    spec_wgt = jnp.fft.rfft(wgt.astype(jnp.float32), n=full, axis=-1)
    conv = jnp.fft.irfft(spec_fil * spec_mix, n=full, axis=-1)[:, :SEQ]
    back = jnp.fft.irfft(jnp.conj(spec_fil) * spec_wgt, n=full, axis=-1)[:, :SEQ]
    grad_fil = jnp.fft.irfft(spec_wgt * jnp.conj(spec_mix), n=full, axis=-1)[:, :SEQ]
    return conv.astype(jnp.float32), back.astype(jnp.float32), grad_fil.astype(jnp.float32)


def reference(query, key_in, value_in, filters, skip_gain, cotangent):
    mixed = (key_in.astype(jnp.float32) * value_in.astype(jnp.float32)).astype(jnp.bfloat16)
    weighted = (cotangent.astype(jnp.float32) * query.astype(jnp.float32)).astype(jnp.bfloat16)
    blocks = C // 256
    conv, back, grad_fil = lax.map(block_spectra, (filters.reshape(blocks, 256, SEQ), mixed.reshape(blocks, 256, SEQ), weighted.reshape(blocks, 256, SEQ)))
    conv = conv.reshape(C, SEQ).astype(jnp.bfloat16).astype(jnp.float32)
    back = back.reshape(C, SEQ).astype(jnp.bfloat16).astype(jnp.float32)
    gain = skip_gain[:, None]
    mixed_f = mixed.astype(jnp.float32)
    weighted_f = weighted.astype(jnp.float32)
    inner = conv + gain * mixed_f
    output = (query.astype(jnp.float32) * inner).astype(jnp.bfloat16)
    grad_query = (cotangent.astype(jnp.float32) * inner).astype(jnp.bfloat16)
    dmixed = back + gain * weighted_f
    grad_key = (dmixed * value_in.astype(jnp.float32)).astype(jnp.bfloat16)
    grad_value = (dmixed * key_in.astype(jnp.float32)).astype(jnp.bfloat16)
    norm_scale = jnp.float32(SEQ) ** -0.5
    grad_filters = grad_fil.reshape(C, SEQ) * norm_scale
    grad_skip = jnp.sum(weighted_f * mixed_f, axis=1) * norm_scale
    return output, grad_query, grad_key, grad_value, grad_filters, grad_skip
```

```python
import functools

import jax
import jax.numpy as jnp
import numpy as np
from jax import lax
from jax.experimental import pallas as pl
from jax.experimental.pallas import tpu as pltpu
from jax.sharding import PartitionSpec as P

F32 = jnp.float32
BF16 = jnp.bfloat16
SIDE = 128
GROUP = 8


def two_terms(values):
    high = np.asarray(values, np.float32).astype(BF16)
    low = (values - high.astype(np.float64)).astype(np.float32).astype(BF16)
    return high, low


def tables():
    index = np.arange(SIDE, dtype=np.float64)
    psi = 2.0 * np.pi * index[:, None] * (index[None, :] + 0.25) / SIDE
    phi = 2.0 * np.pi * (index[:, None] + 0.25) * index[None, :] / (SIDE * SIDE)
    theta = 2.0 * np.pi * ((index[:, None] * index[None, :]) % SIDE) / SIDE
    cos_t, sin_t = np.cos(theta), np.sin(theta)
    fold = np.concatenate([np.cos(psi).T, -np.sin(psi).T], axis=0)
    fold_hi, fold_lo = two_terms(fold)
    spread_hi, spread_lo = two_terms(np.block([[cos_t, -sin_t], [sin_t, cos_t]]))
    gather_hi, gather_lo = two_terms(np.block([[cos_t, sin_t], [-sin_t, cos_t]]) / SIDE)
    unfold_hi, unfold_lo = two_terms(np.concatenate([np.cos(psi), -np.sin(psi)], axis=1) / SIDE)
    return dict(
        fold=np.concatenate([fold_hi, fold_lo], axis=1),
        fold_hi=fold_hi,
        turn_re=np.cos(phi).astype(np.float32),
        turn_im=np.sin(phi).astype(np.float32),
        spread_hi=spread_hi, spread_lo=spread_lo,
        gather_hi=gather_hi, gather_lo=gather_lo,
        unfold_hi=unfold_hi, unfold_lo=unfold_lo,
    )


def dot(lhs, rhs):
    return jnp.dot(lhs, rhs, preferred_element_type=F32)


def split_terms(values):
    high = values.astype(BF16)
    return high, (values - high.astype(F32)).astype(BF16)


def dot_rows(values, hi, lo, passes):
    high, low = split_terms(values)
    total = dot(high, hi)
    if passes >= 2:
        total = total + dot(low, hi)
    if passes >= 3:
        total = total + dot(high, lo)
    return total


def dot_cols(hi, lo, values, passes):
    high, low = split_terms(values)
    total = dot(hi, high)
    if passes >= 2:
        total = total + dot(hi, low)
    if passes >= 3:
        total = total + dot(lo, high)
    return total


def to_spectra(folded, turn_re, turn_im, spread_hi, spread_lo, passes):
    re, im = folded[:SIDE], folded[SIDE:]
    rows = []
    for s in range(2):
        sr, si = re[:, s * SIDE:(s + 1) * SIDE], im[:, s * SIDE:(s + 1) * SIDE]
        rows.append(jnp.concatenate([sr * turn_re + si * turn_im, si * turn_re - sr * turn_im], axis=1))
    return dot_rows(jnp.concatenate(rows, axis=0), spread_hi, spread_lo, passes)


def from_spectra(spectra, turn_re, turn_im, gather_hi, gather_lo, unfold_hi, unfold_lo, passes_g, passes_u):
    part = dot_rows(spectra, gather_hi, gather_lo, passes_g)
    cols = []
    for s in range(2):
        pr, pi = part[s * SIDE:(s + 1) * SIDE, :SIDE], part[s * SIDE:(s + 1) * SIDE, SIDE:]
        cols.append(jnp.concatenate([pr * turn_re - pi * turn_im, pi * turn_re + pr * turn_im], axis=0))
    return dot_cols(unfold_hi, unfold_lo, jnp.concatenate(cols, axis=1), passes_u)


def filter_kernel(fil, fold, fold_hi, turn_re, turn_im, spread_hi, spread_lo, spec, stage):
    for a in range(SIDE):
        stage[a * GROUP:(a + 1) * GROUP, :] = fil[:, a * SIDE:(a + 1) * SIDE]
    tr, ti = turn_re[...], turn_im[...]
    for c in range(0, GROUP, 2):
        pair = jnp.concatenate([stage[pl.ds(c, SIDE, stride=GROUP), :], stage[pl.ds(c + 1, SIDE, stride=GROUP), :]], axis=1)
        high, low = split_terms(pair)
        folded = dot(fold[...], jnp.concatenate([high, high], axis=0)) + dot(fold_hi[...], low)
        out = to_spectra(folded, tr, ti, spread_hi[...], spread_lo[...], 3)
        spec[0, c] = out[:SIDE]
        spec[0, c + 1] = out[SIDE:]


def signal_kernel(passes, got, fil, fold, turn_re, turn_im, spread_hi, spread_lo, gather_hi, gather_lo, unfold_hi, unfold_lo,
                  send, cross, skip, stage, result):
    rows = 2 * GROUP
    stage[...] = got[...].astype(F32).reshape(SIDE * rows, SIDE)
    tr, ti = turn_re[...], turn_im[...]
    for c in range(GROUP):
        mix = stage[pl.ds(c, SIDE, stride=rows), :]
        wgt = stage[pl.ds(c + GROUP, SIDE, stride=rows), :]
        skip[c:c + 1, :] = jnp.sum(mix * wgt, axis=0, keepdims=True)
        pair = jnp.concatenate([mix, wgt], axis=1).astype(BF16)
        folded = dot(fold[...], jnp.concatenate([pair, pair], axis=0))
        both = to_spectra(folded, tr, ti, spread_hi[...], spread_lo[...], passes[0])
        mr, mi = both[:SIDE, :SIDE], both[:SIDE, SIDE:]
        wr, wi = both[SIDE:, :SIDE], both[SIDE:, SIDE:]
        fr, fi = fil[0, c, :, :SIDE], fil[0, c, :, SIDE:]
        cross[0, c, :, :SIDE] = wr * mr + wi * mi
        cross[0, c, :, SIDE:] = wi * mr - wr * mi
        prod = jnp.concatenate([
            jnp.concatenate([fr * mr - fi * mi, fr * mi + fi * mr], axis=1),
            jnp.concatenate([fr * wr + fi * wi, fr * wi - fi * wr], axis=1),
        ], axis=0)
        back = from_spectra(prod, tr, ti, gather_hi[...], gather_lo[...], unfold_hi[...], unfold_lo[...], passes[1], passes[2])
        result[pl.ds(c, SIDE, stride=rows), :] = back[:, :SIDE]
        result[pl.ds(c + GROUP, SIDE, stride=rows), :] = back[:, SIDE:]
    send[...] = result[...].reshape(SIDE, rows, SIDE).astype(BF16)


def grad_kernel(scale, cross, turn_re, turn_im, gather_hi, gather_lo, unfold_hi, unfold_lo, out, stage):
    tr, ti = turn_re[...], turn_im[...]
    for c in range(0, GROUP, 2):
        pair = jnp.concatenate([cross[0, c], cross[0, c + 1]], axis=0)
        back = from_spectra(pair, tr, ti, gather_hi[...], gather_lo[...], unfold_hi[...], unfold_lo[...], 3, 3) * scale
        stage[pl.ds(c, SIDE, stride=GROUP), :] = back[:, :SIDE]
        stage[pl.ds(c + 1, SIDE, stride=GROUP), :] = back[:, SIDE:]
    for a in range(SIDE):
        out[:, a * SIDE:(a + 1) * SIDE] = stage[a * GROUP:(a + 1) * GROUP, :]


def whole(array):
    return pl.BlockSpec(array.shape, lambda g: (0,) * array.ndim)


PARAMS = pltpu.CompilerParams(vmem_limit_bytes=48 * 1024 * 1024)


def cost(rows, moved):
    return pl.CostEstimate(flops=2 * rows * 256 * 256, bytes_accessed=moved, transcendentals=0)


def filter_spectra(filters, tab):
    channels, seq = filters.shape
    groups = channels // GROUP
    ops = [tab[k] for k in ("fold", "fold_hi", "turn_re", "turn_im", "spread_hi", "spread_lo")]
    return pl.pallas_call(
        filter_kernel,
        grid=(groups,),
        in_specs=[pl.BlockSpec((GROUP, seq), lambda g: (g, 0))] + [whole(o) for o in ops],
        out_specs=pl.BlockSpec((1, GROUP, SIDE, 2 * SIDE), lambda g: (g, 0, 0, 0)),
        out_shape=jax.ShapeDtypeStruct((groups, GROUP, SIDE, 2 * SIDE), F32),
        scratch_shapes=[pltpu.VMEM((SIDE * GROUP, SIDE), F32)],
        compiler_params=PARAMS,
        cost_estimate=cost(channels * 5 * SIDE, 6 * channels * seq * 2),
        name="filter_spectra",
    )(filters, *ops)


def convolve(got, spec, tab, passes):
    groups = spec.shape[0]
    channels = groups * GROUP
    ops = [tab[k] for k in ("fold", "turn_re", "turn_im", "spread_hi", "spread_lo", "gather_hi", "gather_lo", "unfold_hi", "unfold_lo")]
    rows = 2 * GROUP
    return pl.pallas_call(
        functools.partial(signal_kernel, passes),
        grid=(groups,),
        in_specs=[pl.BlockSpec((SIDE, rows, SIDE), lambda g: (0, g, 0)),
                  pl.BlockSpec((1, GROUP, SIDE, 2 * SIDE), lambda g: (g, 0, 0, 0))] + [whole(o) for o in ops],
        out_specs=[pl.BlockSpec((SIDE, rows, SIDE), lambda g: (0, g, 0)),
                   pl.BlockSpec((1, GROUP, SIDE, 2 * SIDE), lambda g: (g, 0, 0, 0)),
                   pl.BlockSpec((GROUP, SIDE), lambda g: (g, 0))],
        out_shape=[jax.ShapeDtypeStruct((SIDE, 2 * channels, SIDE), BF16),
                   jax.ShapeDtypeStruct(spec.shape, F32),
                   jax.ShapeDtypeStruct((channels, SIDE), F32)],
        scratch_shapes=[pltpu.VMEM((SIDE * rows, SIDE), F32), pltpu.VMEM((SIDE * rows, SIDE), F32)],
        compiler_params=PARAMS,
        cost_estimate=cost(channels * 17 * SIDE, 12 * channels * SIDE * SIDE),
        name="convolve",
    )(got, spec, *ops)


def filter_gradient(cross, tab, scale):
    groups = cross.shape[0]
    channels = groups * GROUP
    ops = [tab[k] for k in ("turn_re", "turn_im", "gather_hi", "gather_lo", "unfold_hi", "unfold_lo")]
    return pl.pallas_call(
        functools.partial(grad_kernel, scale),
        grid=(groups,),
        in_specs=[pl.BlockSpec((1, GROUP, SIDE, 2 * SIDE), lambda g: (g, 0, 0, 0))] + [whole(o) for o in ops],
        out_specs=pl.BlockSpec((GROUP, SIDE * SIDE), lambda g: (g, 0)),
        out_shape=jax.ShapeDtypeStruct((channels, SIDE * SIDE), F32),
        scratch_shapes=[pltpu.VMEM((SIDE * GROUP, SIDE), F32)],
        compiler_params=PARAMS,
        cost_estimate=cost(channels * 5 * SIDE, 12 * channels * SIDE * SIDE),
        name="filter_gradient",
    )(cross, *ops)


def interleave(first, second):
    parts = [x.reshape(SIDE, -1, GROUP, SIDE) for x in (first, second)]
    return jnp.stack(parts, axis=2).reshape(SIDE, -1, SIDE)


def separate(both):
    parts = both.reshape(SIDE, -1, 2, GROUP, SIDE)
    return parts[:, :, 0].reshape(-1, SIDE), parts[:, :, 1].reshape(-1, SIDE)


def exchange(blocks):
    return lax.all_to_all(blocks, ("node", "local"), split_axis=0, concat_axis=0, tiled=True)


def local(query, key_in, value_in, filters, skip_gain, cotangent):
    tab = tables()
    scale = float(filters.shape[1]) ** -0.5
    mixed = (key_in.astype(F32) * value_in.astype(F32)).astype(BF16)
    weighted = (cotangent.astype(F32) * query.astype(F32)).astype(BF16)
    got = exchange(interleave(mixed, weighted))
    spec = filter_spectra(filters, tab)
    send, cross, skip = convolve(got, spec, tab, (3, 3, 3))
    conv, back = separate(exchange(send))
    grad_filters = filter_gradient(cross, tab, scale)
    grad_skip = jnp.sum(skip, axis=1) * scale
    gain = skip_gain[:, None]
    inner = conv.astype(F32) + gain * mixed.astype(F32)
    output = (query.astype(F32) * inner).astype(BF16)
    grad_query = (cotangent.astype(F32) * inner).astype(BF16)
    dmixed = back.astype(F32) + gain * weighted.astype(F32)
    grad_key = (dmixed * value_in.astype(F32)).astype(BF16)
    grad_value = (dmixed * key_in.astype(F32)).astype(BF16)
    return (output, grad_query, grad_key, grad_value, grad_filters, grad_skip)


def solution(mesh):
    tokens = P(None, ("node", "local"))
    return jax.shard_map(
        local,
        mesh=mesh,
        in_specs=(tokens, tokens, tokens, P(("node", "local"), None), P(), tokens),
        out_specs=(tokens, tokens, tokens, tokens, P(("node", "local"), None), P(("node", "local"))),
        check_vma=False,
    )
```

```python
import functools

import jax
import jax.numpy as jnp
import numpy as np
from jax import lax
from jax.experimental import pallas as pl
from jax.experimental.pallas import tpu as pltpu
from jax.sharding import PartitionSpec as P

F32 = jnp.float32
BF16 = jnp.bfloat16
SIDE = 128
GROUP = 8
OCTET = 8


def two_terms(values):
    high = np.asarray(values, np.float32).astype(BF16)
    low = (values - high.astype(np.float64)).astype(np.float32).astype(BF16)
    return high, low


def tables():
    index = np.arange(SIDE, dtype=np.float64)
    psi = 2.0 * np.pi * index[:, None] * (index[None, :] + 0.25) / SIDE
    phi = 2.0 * np.pi * (index[:, None] + 0.25) * index[None, :] / (SIDE * SIDE)
    theta = 2.0 * np.pi * ((index[:, None] * index[None, :]) % SIDE) / SIDE
    cos_t, sin_t = np.cos(theta), np.sin(theta)
    fold = np.concatenate([np.cos(psi).T, -np.sin(psi).T], axis=0)
    fold_hi, fold_lo = two_terms(fold)
    spread_hi, spread_lo = two_terms(np.block([[cos_t, -sin_t], [sin_t, cos_t]]))
    gather_hi, gather_lo = two_terms(np.block([[cos_t, sin_t], [-sin_t, cos_t]]) / SIDE)
    unfold_hi, unfold_lo = two_terms(np.concatenate([np.cos(psi), -np.sin(psi)], axis=1) / SIDE)
    return dict(
        fold=np.concatenate([fold_hi, fold_lo], axis=1),
        fold_hi=fold_hi,
        turn_re=np.cos(phi).astype(np.float32),
        turn_im=np.sin(phi).astype(np.float32),
        spread_hi=spread_hi, spread_lo=spread_lo,
        gather_hi=gather_hi, gather_lo=gather_lo,
        unfold_hi=unfold_hi, unfold_lo=unfold_lo,
    )


def dot(lhs, rhs):
    return jnp.dot(lhs, rhs, preferred_element_type=F32)


def join(parts, axis):
    return jnp.concatenate(parts, axis=axis)


def fold_pair(pair, exact, fold, fold_hi):
    high = pair.astype(BF16)
    folded = dot(fold[...], join([high, high], 0))
    if not exact:
        folded = folded + dot(fold_hi[...], (pair - high.astype(F32)).astype(BF16))
    return folded


def turn_folded(folded, cos_ref, sin_ref):
    turn_re, turn_im = cos_ref[...], sin_ref[...]
    rows = []
    for s in range(2):
        re, im = folded[:SIDE, s * SIDE:(s + 1) * SIDE], folded[SIDE:, s * SIDE:(s + 1) * SIDE]
        rows.append(join([re * turn_re + im * turn_im, im * turn_re - re * turn_im], 1))
    return join(rows, 0)


def turn_back(part, cos_ref, sin_ref):
    turn_re, turn_im = cos_ref[...], sin_ref[...]
    cols = []
    for s in range(2):
        re, im = part[s * SIDE:(s + 1) * SIDE, :SIDE], part[s * SIDE:(s + 1) * SIDE, SIDE:]
        cols.append(join([re * turn_re - im * turn_im, im * turn_re + re * turn_im], 0))
    return join(cols, 1)


def keep(store, c, values, passes):
    rows = pl.ds(c * 2 * SIDE, 2 * SIDE)
    high = values.astype(BF16)
    store[0, rows, :] = high
    if passes % 2 == 1 and passes > 1:
        store[1, rows, :] = (values - high.astype(F32)).astype(BF16)


def rows_times(store, c, hi, lo, passes):
    rows = pl.ds(c * 2 * SIDE, 2 * SIDE)
    high = store[0, rows, :]
    total = dot(high, hi[...])
    if passes >= 2:
        total = total + dot(high, lo[...])
    if passes >= 3:
        total = total + dot(store[1, rows, :], hi[...])
    return total


def times_rows(hi, lo, store, c, passes):
    rows = pl.ds(c * 2 * SIDE, 2 * SIDE)
    high = store[0, rows, :]
    total = dot(hi[...], high)
    if passes >= 2:
        total = total + dot(lo[...], high)
    if passes >= 3:
        total = total + dot(hi[...], store[1, rows, :])
    return total


def filter_kernel(fil, fold, fold_hi, turn_re, turn_im, spread_hi, spread_lo, spec, stage, turned):
    for a in range(SIDE):
        stage[a * GROUP:(a + 1) * GROUP, :] = fil[:, a * SIDE:(a + 1) * SIDE]
    tr, ti = turn_re, turn_im
    for p in range(GROUP // 2):
        pair = join([stage[pl.ds(2 * p + s, SIDE, stride=GROUP), :] for s in range(2)], 1)
        keep(turned, p, turn_folded(fold_pair(pair, False, fold, fold_hi), tr, ti), 3)
    for p in range(GROUP // 2):
        out = rows_times(turned, p, spread_hi, spread_lo, 3)
        spec[0, 2 * p] = out[:SIDE]
        spec[0, 2 * p + 1] = out[SIDE:]


def load_octets(source, stage):
    for o in range(stage.shape[0]):
        pair = source[:, o // 2 * 2 * OCTET:(o // 2 + 1) * 2 * OCTET, :].astype(F32)
        stage[o] = pair[:, o % 2 * OCTET:(o % 2 + 1) * OCTET].reshape(SIDE * OCTET, SIDE)


def store_octets(result, target):
    for o in range(0, result.shape[0], 2):
        pair = join([result[o + i].reshape(SIDE, OCTET, SIDE) for i in range(2)], 1)
        target[:, o * OCTET:(o + 2) * OCTET, :] = pair.astype(BF16)


def signal_kernel(passes, got, fil, fold, turn_re, turn_im, spread_hi, spread_lo, gather_hi, gather_lo, unfold_hi, unfold_lo,
                  send, cross, skip, stage, result, turned, product, tilted):
    rows = 2 * GROUP
    load_octets(got, stage)
    tr, ti = turn_re, turn_im
    for c in range(GROUP):
        mix = stage[c // OCTET, pl.ds(c % OCTET, SIDE, stride=OCTET), :]
        wgt = stage[(c + GROUP) // OCTET, pl.ds((c + GROUP) % OCTET, SIDE, stride=OCTET), :]
        skip[c:c + 1, :] = jnp.sum(mix * wgt, axis=0, keepdims=True)
        keep(turned, c, turn_folded(fold_pair(join([mix, wgt], 1), True, fold, None), tr, ti), passes[0])
    for c in range(GROUP):
        both = rows_times(turned, c, spread_hi, spread_lo, passes[0])
        mr, mi = both[:SIDE, :SIDE], both[:SIDE, SIDE:]
        wr, wi = both[SIDE:, :SIDE], both[SIDE:, SIDE:]
        fr, fi = fil[0, c, :, :SIDE], fil[0, c, :, SIDE:]
        cross[0, c, :, :SIDE] = wr * mr + wi * mi
        cross[0, c, :, SIDE:] = wi * mr - wr * mi
        keep(product, c, join([
            join([fr * mr - fi * mi, fr * mi + fi * mr], 1),
            join([fr * wr + fi * wi, fr * wi - fi * wr], 1),
        ], 0), passes[1])
    for c in range(GROUP):
        keep(tilted, c, turn_back(rows_times(product, c, gather_hi, gather_lo, passes[1]), tr, ti), passes[2])
    for c in range(GROUP):
        back = times_rows(unfold_hi, unfold_lo, tilted, c, passes[2])
        result[c // OCTET, pl.ds(c % OCTET, SIDE, stride=OCTET), :] = back[:, :SIDE]
        result[(c + GROUP) // OCTET, pl.ds((c + GROUP) % OCTET, SIDE, stride=OCTET), :] = back[:, SIDE:]
    store_octets(result, send)


def grad_kernel(scale, cross, turn_re, turn_im, gather_hi, gather_lo, unfold_hi, unfold_lo, out, stage, product, tilted):
    tr, ti = turn_re, turn_im
    for p in range(GROUP // 2):
        keep(product, p, join([cross[0, 2 * p], cross[0, 2 * p + 1]], 0), 3)
    for p in range(GROUP // 2):
        keep(tilted, p, turn_back(rows_times(product, p, gather_hi, gather_lo, 3), tr, ti), 3)
    for p in range(GROUP // 2):
        back = times_rows(unfold_hi, unfold_lo, tilted, p, 3) * scale
        for s in range(2):
            stage[pl.ds(2 * p + s, SIDE, stride=GROUP), :] = back[:, s * SIDE:(s + 1) * SIDE]
    for a in range(SIDE):
        out[:, a * SIDE:(a + 1) * SIDE] = stage[a * GROUP:(a + 1) * GROUP, :]


def held(signals):
    return pltpu.VMEM((2, signals * SIDE, 2 * SIDE), BF16)


def whole(array):
    return pl.BlockSpec(array.shape, lambda g: (0,) * array.ndim)


FAR = pl.BlockSpec(memory_space=pltpu.HBM)
NEAR = pl.BlockSpec(memory_space=pltpu.VMEM)


def granted(mib):
    return pltpu.CompilerParams(vmem_limit_bytes=mib * 1024 * 1024)


PARAMS = granted(60)


def cost(rows, moved):
    return pl.CostEstimate(flops=2 * rows * 256 * 256, bytes_accessed=moved, transcendentals=0)


def filter_spectra(filters, tab):
    channels, seq = filters.shape
    groups = channels // GROUP
    ops = [tab[k] for k in ("fold", "fold_hi", "turn_re", "turn_im", "spread_hi", "spread_lo")]
    return pl.pallas_call(
        filter_kernel,
        grid=(groups,),
        in_specs=[pl.BlockSpec((GROUP, seq), lambda g: (g, 0))] + [whole(o) for o in ops],
        out_specs=pl.BlockSpec((1, GROUP, SIDE, 2 * SIDE), lambda g: (g, 0, 0, 0)),
        out_shape=jax.ShapeDtypeStruct((groups, GROUP, SIDE, 2 * SIDE), F32),
        scratch_shapes=[pltpu.VMEM((SIDE * GROUP, SIDE), F32), held(GROUP)],
        compiler_params=PARAMS,
        cost_estimate=cost(channels * 5 * SIDE, 6 * channels * seq * 2),
        name="filter_spectra",
    )(filters, *ops)


def convolve(got, spec, tab, passes):
    groups = spec.shape[0]
    channels = groups * GROUP
    ops = [tab[k] for k in ("fold", "turn_re", "turn_im", "spread_hi", "spread_lo", "gather_hi", "gather_lo", "unfold_hi", "unfold_lo")]
    rows = 2 * GROUP
    return pl.pallas_call(
        functools.partial(signal_kernel, passes),
        grid=(groups,),
        in_specs=[pl.BlockSpec((SIDE, rows, SIDE), lambda g: (0, g, 0)),
                  pl.BlockSpec((1, GROUP, SIDE, 2 * SIDE), lambda g: (g, 0, 0, 0))] + [whole(o) for o in ops],
        out_specs=[pl.BlockSpec((SIDE, rows, SIDE), lambda g: (0, g, 0)),
                   pl.BlockSpec((1, GROUP, SIDE, 2 * SIDE), lambda g: (g, 0, 0, 0)),
                   pl.BlockSpec((GROUP, SIDE), lambda g: (g, 0))],
        out_shape=[pltpu.HBM((SIDE, 2 * channels, SIDE), BF16),
                   pltpu.HBM(spec.shape, F32),
                   jax.ShapeDtypeStruct((channels, SIDE), F32)],
        scratch_shapes=[pltpu.VMEM((rows // OCTET, SIDE * OCTET, SIDE), F32)] * 2 + [held(2 * GROUP)] * 3,
        compiler_params=granted(48),
        cost_estimate=cost(channels * 17 * SIDE, 12 * channels * SIDE * SIDE),
        name="convolve",
    )(got, spec, *ops)


def filter_gradient(cross, tab, scale):
    groups = cross.shape[0]
    channels = groups * GROUP
    ops = [tab[k] for k in ("turn_re", "turn_im", "gather_hi", "gather_lo", "unfold_hi", "unfold_lo")]
    return pl.pallas_call(
        functools.partial(grad_kernel, scale),
        grid=(groups,),
        in_specs=[pl.BlockSpec((1, GROUP, SIDE, 2 * SIDE), lambda g: (g, 0, 0, 0))] + [whole(o) for o in ops],
        out_specs=pl.BlockSpec((GROUP, SIDE * SIDE), lambda g: (g, 0)),
        out_shape=jax.ShapeDtypeStruct((channels, SIDE * SIDE), F32),
        scratch_shapes=[pltpu.VMEM((SIDE * GROUP, SIDE), F32), held(GROUP), held(GROUP)],
        compiler_params=PARAMS,
        cost_estimate=cost(channels * 5 * SIDE, 12 * channels * SIDE * SIDE),
        name="filter_gradient",
    )(cross, *ops)


PIECES = 8


def chunk(array, i):
    size = array.shape[0] // PIECES
    return array.at[pl.ds(i * size, size)]


def fetches(sources, stores, sems):
    return [[pltpu.make_async_copy(chunk(s, i), chunk(d, i), sems.at[j, i]) for j, (s, d) in enumerate(zip(sources, stores))]
            for i in range(PIECES)]


def products_kernel(query, key_in, value_in, cotangent, out, q, k, v, c, both, in_sem, out_sem):
    loads = fetches((query, key_in, value_in, cotangent), (q, k, v, c), in_sem)
    stores = [s[0] for s in fetches((both,), (out,), out_sem)]
    for group in loads:
        for copy in group:
            copy.start()
    for i in range(PIECES):
        for copy in loads[i]:
            copy.wait()
        qi, ki, vi, ci = [chunk(x, i)[...].astype(F32) for x in (q, k, v, c)]
        pair = jnp.stack([x.reshape(-1, GROUP, SIDE) for x in (ki * vi, ci * qi)], axis=1)
        chunk(both, i)[...] = pair.reshape(chunk(both, i).shape).astype(BF16)
        stores[i].start()
    for copy in stores:
        copy.wait()


def products(query, key_in, value_in, cotangent, own):
    channels = query.shape[0]
    sent = (channels // own, 2 * own, SIDE)
    return pl.pallas_call(
        products_kernel,
        in_specs=[FAR] * 4,
        out_specs=FAR,
        out_shape=jax.ShapeDtypeStruct(sent, BF16),
        scratch_shapes=[pltpu.VMEM(query.shape, BF16)] * 4 + [pltpu.VMEM(sent, BF16)]
        + [pltpu.SemaphoreType.DMA((4, PIECES)), pltpu.SemaphoreType.DMA((1, PIECES))],
        compiler_params=PARAMS,
        cost_estimate=pl.CostEstimate(flops=2 * channels * SIDE, bytes_accessed=12 * channels * SIDE, transcendentals=0),
        name="products",
    )(query, key_in, value_in, cotangent)


def finish_kernel(query, key_in, value_in, cotangent, got, gain, output, grad_query, grad_key, grad_value,
                  q, k, v, c, spread, out_a, out_b, out_c, out_d, in_sem, out_sem):
    results = (out_a, out_b, out_c, out_d)
    loads = fetches((query, key_in, value_in, cotangent), (q, k, v, c), in_sem)
    stores = fetches(results, (output, grad_query, grad_key, grad_value), out_sem)
    for group in loads:
        for copy in group:
            copy.start()
    for i in range(gain.shape[0]):
        spread[i * SIDE:(i + 1) * SIDE, :] = jnp.broadcast_to(gain[i:i + 1, :], (SIDE, SIDE)).T
    for i in range(PIECES):
        for copy in loads[i]:
            copy.wait()
        qi, ki, vi, ci, pair = [chunk(x, i)[...].astype(F32) for x in (q, k, v, c, got)]
        pair = pair.reshape(-1, 2, GROUP, SIDE)
        conv, back = pair[:, 0].reshape(qi.shape), pair[:, 1].reshape(qi.shape)
        g = chunk(spread, i)[...]
        inner = conv + g * (ki * vi).astype(BF16).astype(F32)
        dmixed = back + g * (ci * qi).astype(BF16).astype(F32)
        for store, value in zip(results, (qi * inner, ci * inner, dmixed * vi, dmixed * ki)):
            chunk(store, i)[...] = value.astype(BF16)
        for copy in stores[i]:
            copy.start()
    for group in stores:
        for copy in group:
            copy.wait()


def finish(query, key_in, value_in, cotangent, got, gain):
    channels = query.shape[0]
    return pl.pallas_call(
        finish_kernel,
        in_specs=[FAR] * 4 + [NEAR] * 2,
        out_specs=[FAR] * 4,
        out_shape=[jax.ShapeDtypeStruct(query.shape, BF16)] * 4,
        scratch_shapes=[pltpu.VMEM(query.shape, BF16)] * 4 + [pltpu.VMEM(query.shape, F32)]
        + [pltpu.VMEM(query.shape, BF16)] * 4
        + [pltpu.SemaphoreType.DMA((4, PIECES)), pltpu.SemaphoreType.DMA((4, PIECES))],
        compiler_params=granted(61),
        cost_estimate=pl.CostEstimate(flops=10 * channels * SIDE, bytes_accessed=20 * channels * SIDE, transcendentals=0),
        name="finish",
    )(query, key_in, value_in, cotangent, got, gain)


def exchange(blocks):
    return lax.all_to_all(blocks, ("node", "local"), split_axis=0, concat_axis=0, tiled=True)


def local(query, key_in, value_in, filters, skip_gain, cotangent):
    tab = tables()
    scale = float(filters.shape[1]) ** -0.5
    got = exchange(products(query, key_in, value_in, cotangent, filters.shape[0]))
    spec = filter_spectra(filters, tab)
    gain = skip_gain.reshape(-1, SIDE)
    send, cross, skip = convolve(got, spec, tab, (3, 3, 3))
    back = exchange(send)
    grad_filters = filter_gradient(cross, tab, scale)
    grad_skip = jnp.sum(skip.reshape(-1, SIDE), axis=1) * scale
    return (*finish(query, key_in, value_in, cotangent, back, gain), grad_filters, grad_skip)


def solution(mesh):
    tokens = P(None, ("node", "local"))
    return jax.shard_map(
        local,
        mesh=mesh,
        in_specs=(tokens, tokens, tokens, P(("node", "local"), None), P(), tokens),
        out_specs=(tokens, tokens, tokens, tokens, P(("node", "local"), None), P(("node", "local"))),
        check_vma=False,
    )
```

```python
import functools

import jax
import jax.numpy as jnp
import numpy as np
from jax import lax
from jax.experimental import pallas as pl
from jax.experimental.pallas import tpu as pltpu
from jax.sharding import PartitionSpec as P

F32 = jnp.float32
BF16 = jnp.bfloat16
SIDE = 128
GROUP = 8
OCTET = 8


def two_terms(values):
    high = np.asarray(values, np.float32).astype(BF16)
    low = (values - high.astype(np.float64)).astype(np.float32).astype(BF16)
    return high, low


def tables():
    index = np.arange(SIDE, dtype=np.float64)
    psi = 2.0 * np.pi * index[:, None] * (index[None, :] + 0.25) / SIDE
    phi = 2.0 * np.pi * (index[:, None] + 0.25) * index[None, :] / (SIDE * SIDE)
    theta = 2.0 * np.pi * ((index[:, None] * index[None, :]) % SIDE) / SIDE
    cos_t, sin_t = np.cos(theta), np.sin(theta)
    fold = np.concatenate([np.cos(psi).T, -np.sin(psi).T], axis=0)
    fold_hi, fold_lo = two_terms(fold)
    spread_hi, spread_lo = two_terms(np.block([[cos_t, -sin_t], [sin_t, cos_t]]))
    gather_hi, gather_lo = two_terms(np.block([[cos_t, sin_t], [-sin_t, cos_t]]) / SIDE)
    unfold_hi, unfold_lo = two_terms(np.concatenate([np.cos(psi), -np.sin(psi)], axis=1) / SIDE)
    return dict(
        fold=np.concatenate([fold_hi, fold_lo], axis=1),
        fold_hi=fold_hi,
        turn_re=np.cos(phi).astype(np.float32),
        turn_im=np.sin(phi).astype(np.float32),
        spread_hi=spread_hi, spread_lo=spread_lo,
        gather_hi=gather_hi, gather_lo=gather_lo,
        unfold_hi=unfold_hi, unfold_lo=unfold_lo,
    )


def dot(lhs, rhs):
    return jnp.dot(lhs, rhs, preferred_element_type=F32)


def join(parts, axis):
    return jnp.concatenate(parts, axis=axis)


def fold_pair(pair, exact, fold, fold_hi):
    high = pair.astype(BF16)
    folded = dot(fold[...], join([high, high], 0))
    if not exact:
        folded = folded + dot(fold_hi[...], (pair - high.astype(F32)).astype(BF16))
    return folded


def turn_folded(folded, cos_ref, sin_ref):
    turn_re, turn_im = cos_ref[...], sin_ref[...]
    rows = []
    for s in range(2):
        re, im = folded[:SIDE, s * SIDE:(s + 1) * SIDE], folded[SIDE:, s * SIDE:(s + 1) * SIDE]
        rows.append(join([re * turn_re + im * turn_im, im * turn_re - re * turn_im], 1))
    return join(rows, 0)


def turn_back(part, cos_ref, sin_ref):
    turn_re, turn_im = cos_ref[...], sin_ref[...]
    cols = []
    for s in range(2):
        re, im = part[s * SIDE:(s + 1) * SIDE, :SIDE], part[s * SIDE:(s + 1) * SIDE, SIDE:]
        cols.append(join([re * turn_re - im * turn_im, im * turn_re + re * turn_im], 0))
    return join(cols, 1)


def keep(store, c, values, passes):
    rows = pl.ds(c * 2 * SIDE, 2 * SIDE)
    high = values.astype(BF16)
    store[0, rows, :] = high
    if passes % 2 == 1 and passes > 1:
        store[1, rows, :] = (values - high.astype(F32)).astype(BF16)


def rows_times(store, c, hi, lo, passes):
    rows = pl.ds(c * 2 * SIDE, 2 * SIDE)
    high = store[0, rows, :]
    lhs, rhs = [high], [hi[...]]
    if passes >= 2:
        lhs, rhs = lhs + [high], rhs + [lo[...]]
    if passes >= 3:
        lhs, rhs = lhs + [store[1, rows, :]], rhs + [hi[...]]
    return dot(join(lhs, 1), join(rhs, 0))


def times_rows(hi, lo, store, c, passes):
    rows = pl.ds(c * 2 * SIDE, 2 * SIDE)
    high = store[0, rows, :]
    lhs, rhs = [hi[...]], [high]
    if passes >= 2:
        lhs, rhs = lhs + [lo[...]], rhs + [high]
    if passes >= 3:
        lhs, rhs = lhs + [hi[...]], rhs + [store[1, rows, :]]
    return dot(join(lhs, 1), join(rhs, 0))


def filter_kernel(fil, fold, fold_hi, turn_re, turn_im, spread_hi, spread_lo, spec, stage, turned):
    for a in range(SIDE):
        stage[a * GROUP:(a + 1) * GROUP, :] = fil[:, a * SIDE:(a + 1) * SIDE]
    tr, ti = turn_re, turn_im
    for p in range(GROUP // 2):
        pair = join([stage[pl.ds(2 * p + s, SIDE, stride=GROUP), :] for s in range(2)], 1)
        keep(turned, p, turn_folded(fold_pair(pair, False, fold, fold_hi), tr, ti), 3)
    for p in range(GROUP // 2):
        out = rows_times(turned, p, spread_hi, spread_lo, 3)
        spec[0, 2 * p] = out[:SIDE]
        spec[0, 2 * p + 1] = out[SIDE:]


def load_octets(source, stage):
    for o in range(stage.shape[0]):
        pair = source[:, o // 2 * 2 * OCTET:(o // 2 + 1) * 2 * OCTET, :].astype(F32)
        stage[o] = pair[:, o % 2 * OCTET:(o % 2 + 1) * OCTET].reshape(SIDE * OCTET, SIDE)


def store_octets(result, target):
    for o in range(0, result.shape[0], 2):
        pair = join([result[o + i].reshape(SIDE, OCTET, SIDE) for i in range(2)], 1)
        target[:, o * OCTET:(o + 2) * OCTET, :] = pair.astype(BF16)


def signal_kernel(passes, got, fil, fold, turn_re, turn_im, spread_hi, spread_lo, gather_hi, gather_lo, unfold_hi, unfold_lo,
                  send, cross, skip, stage, result, turned, product, tilted):
    rows = 2 * GROUP
    load_octets(got, stage)
    tr, ti = turn_re, turn_im
    for c in range(GROUP):
        mix = stage[c // OCTET, pl.ds(c % OCTET, SIDE, stride=OCTET), :]
        wgt = stage[(c + GROUP) // OCTET, pl.ds((c + GROUP) % OCTET, SIDE, stride=OCTET), :]
        skip[c:c + 1, :] = jnp.sum(mix * wgt, axis=0, keepdims=True)
        keep(turned, c, turn_folded(fold_pair(join([mix, wgt], 1), True, fold, None), tr, ti), passes[0])
    for c in range(GROUP):
        both = rows_times(turned, c, spread_hi, spread_lo, passes[0])
        mr, mi = both[:SIDE, :SIDE], both[:SIDE, SIDE:]
        wr, wi = both[SIDE:, :SIDE], both[SIDE:, SIDE:]
        fr, fi = fil[0, c, :, :SIDE], fil[0, c, :, SIDE:]
        cross[0, c, :, :SIDE] = (wr * mr + wi * mi).astype(BF16)
        cross[0, c, :, SIDE:] = (wi * mr - wr * mi).astype(BF16)
        keep(product, c, join([
            join([fr * mr - fi * mi, fr * mi + fi * mr], 1),
            join([fr * wr + fi * wi, fr * wi - fi * wr], 1),
        ], 0), passes[1])
    for c in range(GROUP):
        keep(tilted, c, turn_back(rows_times(product, c, gather_hi, gather_lo, passes[1]), tr, ti), passes[2])
    for c in range(GROUP):
        back = times_rows(unfold_hi, unfold_lo, tilted, c, passes[2])
        result[c // OCTET, pl.ds(c % OCTET, SIDE, stride=OCTET), :] = back[:, :SIDE]
        result[(c + GROUP) // OCTET, pl.ds((c + GROUP) % OCTET, SIDE, stride=OCTET), :] = back[:, SIDE:]
    store_octets(result, send)


def grad_kernel(scale, cross, turn_re, turn_im, gather_hi, gather_lo, unfold_hi, unfold_lo, out, stage, tilted):
    tr, ti = turn_re, turn_im
    pairs = cross.reshape(1, GROUP * SIDE, 2 * SIDE)
    for p in range(GROUP // 2):
        keep(tilted, p, turn_back(rows_times(pairs, p, gather_hi, gather_lo, 2), tr, ti), 3)
    for p in range(GROUP // 2):
        back = times_rows(unfold_hi, unfold_lo, tilted, p, 3) * scale
        for s in range(2):
            stage[pl.ds(2 * p + s, SIDE, stride=GROUP), :] = back[:, s * SIDE:(s + 1) * SIDE]
    for a in range(SIDE):
        out[:, a * SIDE:(a + 1) * SIDE] = stage[a * GROUP:(a + 1) * GROUP, :]


def held(signals):
    return pltpu.VMEM((2, signals * SIDE, 2 * SIDE), BF16)


def whole(array):
    return pl.BlockSpec(array.shape, lambda g: (0,) * array.ndim)


FAR = pl.BlockSpec(memory_space=pltpu.HBM)
NEAR = pl.BlockSpec(memory_space=pltpu.VMEM)


def granted(mib):
    return pltpu.CompilerParams(vmem_limit_bytes=mib * 1024 * 1024)


PARAMS = granted(60)


def cost(rows, moved):
    return pl.CostEstimate(flops=2 * rows * 256 * 256, bytes_accessed=moved, transcendentals=0)


def filter_spectra(filters, tab):
    channels, seq = filters.shape
    groups = channels // GROUP
    ops = [tab[k] for k in ("fold", "fold_hi", "turn_re", "turn_im", "spread_hi", "spread_lo")]
    return pl.pallas_call(
        filter_kernel,
        grid=(groups,),
        in_specs=[pl.BlockSpec((GROUP, seq), lambda g: (g, 0))] + [whole(o) for o in ops],
        out_specs=pl.BlockSpec((1, GROUP, SIDE, 2 * SIDE), lambda g: (g, 0, 0, 0)),
        out_shape=jax.ShapeDtypeStruct((groups, GROUP, SIDE, 2 * SIDE), F32),
        scratch_shapes=[pltpu.VMEM((SIDE * GROUP, SIDE), F32), held(GROUP)],
        compiler_params=PARAMS,
        cost_estimate=cost(channels * 5 * SIDE, 6 * channels * seq * 2),
        name="filter_spectra",
    )(filters, *ops)


def convolve(got, spec, tab, passes):
    groups = spec.shape[0]
    channels = groups * GROUP
    ops = [tab[k] for k in ("fold", "turn_re", "turn_im", "spread_hi", "spread_lo", "gather_hi", "gather_lo", "unfold_hi", "unfold_lo")]
    rows = 2 * GROUP
    return pl.pallas_call(
        functools.partial(signal_kernel, passes),
        grid=(groups,),
        in_specs=[pl.BlockSpec((SIDE, rows, SIDE), lambda g: (0, g, 0)),
                  pl.BlockSpec((1, GROUP, SIDE, 2 * SIDE), lambda g: (g, 0, 0, 0))] + [whole(o) for o in ops],
        out_specs=[pl.BlockSpec((SIDE, rows, SIDE), lambda g: (0, g, 0)),
                   pl.BlockSpec((1, GROUP, SIDE, 2 * SIDE), lambda g: (g, 0, 0, 0)),
                   pl.BlockSpec((GROUP, SIDE), lambda g: (g, 0))],
        out_shape=[pltpu.HBM((SIDE, 2 * channels, SIDE), BF16),
                   pltpu.HBM(spec.shape, BF16),
                   jax.ShapeDtypeStruct((channels, SIDE), F32)],
        scratch_shapes=[pltpu.VMEM((rows // OCTET, SIDE * OCTET, SIDE), F32)] * 2 + [held(2 * GROUP)] * 3,
        compiler_params=granted(48),
        cost_estimate=cost(channels * 17 * SIDE, 12 * channels * SIDE * SIDE),
        name="convolve",
    )(got, spec, *ops)


def filter_gradient(cross, tab, scale):
    groups = cross.shape[0]
    channels = groups * GROUP
    ops = [tab[k] for k in ("turn_re", "turn_im", "gather_hi", "gather_lo", "unfold_hi", "unfold_lo")]
    return pl.pallas_call(
        functools.partial(grad_kernel, scale),
        grid=(groups,),
        in_specs=[pl.BlockSpec((1, GROUP, SIDE, 2 * SIDE), lambda g: (g, 0, 0, 0))] + [whole(o) for o in ops],
        out_specs=pl.BlockSpec((GROUP, SIDE * SIDE), lambda g: (g, 0)),
        out_shape=jax.ShapeDtypeStruct((channels, SIDE * SIDE), F32),
        scratch_shapes=[pltpu.VMEM((SIDE * GROUP, SIDE), F32), held(GROUP)],
        compiler_params=PARAMS,
        cost_estimate=cost(channels * 5 * SIDE, 12 * channels * SIDE * SIDE),
        name="filter_gradient",
    )(cross, *ops)


PIECES = 4


def chunk(array, i):
    size = array.shape[0] // PIECES
    return array.at[pl.ds(i * size, size)]


def fetches(sources, stores, sems):
    return [[pltpu.make_async_copy(chunk(s, i), chunk(d, i), sems.at[j, i]) for j, (s, d) in enumerate(zip(sources, stores))]
            for i in range(PIECES)]


def products_kernel(query, key_in, value_in, cotangent, out, q, k, v, c, both, in_sem, out_sem):
    loads = fetches((query, key_in, value_in, cotangent), (q, k, v, c), in_sem)
    stores = [s[0] for s in fetches((both,), (out,), out_sem)]
    for group in loads:
        for copy in group:
            copy.start()
    for i in range(PIECES):
        for copy in loads[i]:
            copy.wait()
        qi, ki, vi, ci = [chunk(x, i)[...].astype(F32) for x in (q, k, v, c)]
        pair = jnp.stack([x.reshape(-1, GROUP, SIDE) for x in (ki * vi, ci * qi)], axis=1)
        chunk(both, i)[...] = pair.reshape(chunk(both, i).shape).astype(BF16)
        stores[i].start()
    for copy in stores:
        copy.wait()


def products(query, key_in, value_in, cotangent, own):
    channels = query.shape[0]
    sent = (channels // own, 2 * own, SIDE)
    return pl.pallas_call(
        products_kernel,
        in_specs=[FAR] * 4,
        out_specs=FAR,
        out_shape=jax.ShapeDtypeStruct(sent, BF16),
        scratch_shapes=[pltpu.VMEM(query.shape, BF16)] * 4 + [pltpu.VMEM(sent, BF16)]
        + [pltpu.SemaphoreType.DMA((4, PIECES)), pltpu.SemaphoreType.DMA((1, PIECES))],
        compiler_params=PARAMS,
        cost_estimate=pl.CostEstimate(flops=2 * channels * SIDE, bytes_accessed=12 * channels * SIDE, transcendentals=0),
        name="products",
    )(query, key_in, value_in, cotangent)


def finish_kernel(query, key_in, value_in, cotangent, got, gain, output, grad_query, grad_key, grad_value,
                  c, both, spread, out_a, out_b, out_c, out_d, in_sem, out_sem):
    results = (out_a, out_b, out_c, out_d)
    loads = fetches((cotangent, got), (c, both), in_sem)
    stores = fetches(results, (output, grad_query, grad_key, grad_value), out_sem)
    for group in loads:
        for copy in group:
            copy.start()
    for i in range(gain.shape[0]):
        spread[i * SIDE:(i + 1) * SIDE, :] = jnp.broadcast_to(gain[i:i + 1, :], (SIDE, SIDE)).T
    for i in range(PIECES):
        for copy in loads[i]:
            copy.wait()
        qi, ki, vi, ci, pair = [chunk(x, i)[...].astype(F32) for x in (query, key_in, value_in, c, both)]
        pair = pair.reshape(-1, 2, GROUP, SIDE)
        conv, back = pair[:, 0].reshape(qi.shape), pair[:, 1].reshape(qi.shape)
        g = chunk(spread, i)[...]
        inner = conv + g * (ki * vi).astype(BF16).astype(F32)
        dmixed = back + g * (ci * qi).astype(BF16).astype(F32)
        for store, value in zip(results, (qi * inner, ci * inner, dmixed * vi, dmixed * ki)):
            chunk(store, i)[...] = value.astype(BF16)
        for copy in stores[i]:
            copy.start()
    for group in stores:
        for copy in group:
            copy.wait()


def finish(query, key_in, value_in, cotangent, got, gain):
    channels = query.shape[0]
    return pl.pallas_call(
        finish_kernel,
        in_specs=[NEAR] * 3 + [FAR] * 2 + [NEAR],
        out_specs=[FAR] * 4,
        out_shape=[jax.ShapeDtypeStruct(query.shape, BF16)] * 4,
        scratch_shapes=[pltpu.VMEM(query.shape, BF16), pltpu.VMEM(got.shape, BF16), pltpu.VMEM(query.shape, F32)]
        + [pltpu.VMEM(query.shape, BF16)] * 4
        + [pltpu.SemaphoreType.DMA((2, PIECES)), pltpu.SemaphoreType.DMA((4, PIECES))],
        compiler_params=granted(48),
        cost_estimate=pl.CostEstimate(flops=10 * channels * SIDE, bytes_accessed=20 * channels * SIDE, transcendentals=0),
        name="finish",
    )(query, key_in, value_in, cotangent, got, gain)


def exchange(blocks):
    return lax.all_to_all(blocks, ("node", "local"), split_axis=0, concat_axis=0, tiled=True)


def local(query, key_in, value_in, filters, skip_gain, cotangent):
    tab = tables()
    scale = float(filters.shape[1]) ** -0.5
    got = exchange(products(query, key_in, value_in, cotangent, filters.shape[0]))
    spec = filter_spectra(filters, tab)
    gain = skip_gain.reshape(-1, SIDE)
    send, cross, skip = convolve(got, spec, tab, (2, 2, 2))
    back = exchange(send)
    grad_filters = filter_gradient(cross, tab, scale)
    grad_skip = jnp.sum(skip.reshape(-1, SIDE), axis=1) * scale
    return (*finish(query, key_in, value_in, cotangent, back, gain), grad_filters, grad_skip)


def solution(mesh):
    tokens = P(None, ("node", "local"))
    return jax.shard_map(
        local,
        mesh=mesh,
        in_specs=(tokens, tokens, tokens, P(("node", "local"), None), P(), tokens),
        out_specs=(tokens, tokens, tokens, tokens, P(("node", "local"), None), P(("node", "local"))),
        check_vma=False,
    )
```

```python
import functools

import jax
import jax.numpy as jnp
import numpy as np
from jax import lax
from jax.experimental import pallas as pl
from jax.experimental.pallas import tpu as pltpu
from jax.sharding import PartitionSpec as P

F32 = jnp.float32
BF16 = jnp.bfloat16
SIDE = 128
TILT = 1.62305
GROUP = 8
OCTET = 8


def two_terms(values):
    high = np.asarray(values, np.float32).astype(BF16)
    low = (values - high.astype(np.float64)).astype(np.float32).astype(BF16)
    return high, low


def one_term(values):
    high = (values * TILT).astype(np.float32).astype(BF16)
    wide = high.astype(np.float64)
    return high, float((wide * values).sum() / (values * values).sum())


def tables():
    index = np.arange(SIDE, dtype=np.float64)
    psi = 2.0 * np.pi * index[:, None] * (index[None, :] + 0.25) / SIDE
    phi = 2.0 * np.pi * (index[:, None] + 0.25) * index[None, :] / (SIDE * SIDE)
    theta = 2.0 * np.pi * ((index[:, None] * index[None, :]) % SIDE) / SIDE
    cos_t, sin_t = np.cos(theta), np.sin(theta)
    fold = np.concatenate([np.cos(psi).T, -np.sin(psi).T], axis=0)
    fold_hi, fold_lo = two_terms(fold)
    spread_hi, spread_lo = two_terms(np.block([[cos_t, -sin_t], [sin_t, cos_t]]))
    gather_hi, gather_lo = two_terms(np.block([[cos_t, sin_t], [-sin_t, cos_t]]) / SIDE)
    unfold = np.concatenate([np.cos(psi), -np.sin(psi)], axis=1) / SIDE
    unfold_hi, unfold_lo = two_terms(unfold)
    spread_one, spread_gain = one_term(np.block([[cos_t, -sin_t], [sin_t, cos_t]]))
    gather_one, gather_gain = one_term(np.block([[cos_t, sin_t], [-sin_t, cos_t]]) / SIDE)
    level_hi, level_lo = two_terms(unfold / (spread_gain * gather_gain))
    return dict(
        fold=np.concatenate([fold_hi, fold_lo], axis=1),
        fold_hi=fold_hi,
        turn_re=np.cos(phi).astype(np.float32),
        turn_im=np.sin(phi).astype(np.float32),
        spread_hi=spread_hi, spread_lo=spread_lo,
        gather_hi=gather_hi, gather_lo=gather_lo,
        unfold_hi=unfold_hi, unfold_lo=unfold_lo,
        spread_one=spread_one, gather_one=gather_one,
        level_hi=level_hi, level_lo=level_lo, cross_gain=spread_gain**2,
    )


def dot(lhs, rhs):
    return jnp.dot(lhs, rhs, preferred_element_type=F32)


def join(parts, axis):
    return jnp.concatenate(parts, axis=axis)


def fold_pair(pair, exact, fold, fold_hi):
    high = pair.astype(BF16)
    folded = dot(fold[...], join([high, high], 0))
    if not exact:
        folded = folded + dot(fold_hi[...], (pair - high.astype(F32)).astype(BF16))
    return folded


def turn_folded(folded, cos_ref, sin_ref):
    turn_re, turn_im = cos_ref[...], sin_ref[...]
    rows = []
    for s in range(2):
        re, im = folded[:SIDE, s * SIDE:(s + 1) * SIDE], folded[SIDE:, s * SIDE:(s + 1) * SIDE]
        rows.append(join([re * turn_re + im * turn_im, im * turn_re - re * turn_im], 1))
    return join(rows, 0)


def turn_back(part, cos_ref, sin_ref):
    turn_re, turn_im = cos_ref[...], sin_ref[...]
    cols = []
    for s in range(2):
        re, im = part[s * SIDE:(s + 1) * SIDE, :SIDE], part[s * SIDE:(s + 1) * SIDE, SIDE:]
        cols.append(join([re * turn_re - im * turn_im, im * turn_re + re * turn_im], 0))
    return join(cols, 1)


def keep(store, c, values, passes):
    rows = pl.ds(c * 2 * SIDE, 2 * SIDE)
    high = values.astype(BF16)
    store[0, rows, :] = high
    if passes % 2 == 1 and passes > 1:
        store[1, rows, :] = (values - high.astype(F32)).astype(BF16)


def rows_times(store, c, hi, lo, passes):
    rows = pl.ds(c * 2 * SIDE, 2 * SIDE)
    high = store[0, rows, :]
    lhs, rhs = [high], [hi[...]]
    if passes >= 2:
        lhs, rhs = lhs + [high], rhs + [lo[...]]
    if passes >= 3:
        lhs, rhs = lhs + [store[1, rows, :]], rhs + [hi[...]]
    return dot(join(lhs, 1), join(rhs, 0))


def times_rows(hi, lo, store, c, passes):
    rows = pl.ds(c * 2 * SIDE, 2 * SIDE)
    high = store[0, rows, :]
    if passes == 2:
        both = dot(join([hi[...], lo[...]], 0), high)
        return both[:SIDE] + both[SIDE:]
    lhs, rhs = [hi[...]], [high]
    if passes >= 2:
        lhs, rhs = lhs + [lo[...]], rhs + [high]
    if passes >= 3:
        lhs, rhs = lhs + [hi[...]], rhs + [store[1, rows, :]]
    return dot(join(lhs, 1), join(rhs, 0))


def filter_kernel(fil, fold, fold_hi, turn_re, turn_im, spread_hi, spread_lo, spec, stage, turned):
    for a in range(SIDE):
        stage[a * GROUP:(a + 1) * GROUP, :] = fil[:, a * SIDE:(a + 1) * SIDE]
    tr, ti = turn_re, turn_im
    for p in range(GROUP // 2):
        pair = join([stage[pl.ds(2 * p + s, SIDE, stride=GROUP), :] for s in range(2)], 1)
        keep(turned, p, turn_folded(fold_pair(pair, False, fold, fold_hi), tr, ti), 3)
    for p in range(GROUP // 2):
        out = rows_times(turned, p, spread_hi, spread_lo, 3)
        spec[0, 2 * p] = out[:SIDE]
        spec[0, 2 * p + 1] = out[SIDE:]


def load_octets(source, stage):
    for o in range(stage.shape[0]):
        pair = source[:, o // 2 * 2 * OCTET:(o // 2 + 1) * 2 * OCTET, :].astype(F32)
        stage[o] = pair[:, o % 2 * OCTET:(o % 2 + 1) * OCTET].reshape(SIDE * OCTET, SIDE)


def store_octets(result, target):
    for o in range(0, result.shape[0], 2):
        pair = join([result[o + i].reshape(SIDE, OCTET, SIDE) for i in range(2)], 1)
        target[:, o * OCTET:(o + 2) * OCTET, :] = pair.astype(BF16)


def signal_kernel(got, fil, fold, turn_re, turn_im, spread, gather, unfold_hi, unfold_lo,
                  send, cross, skip, spectra, stage, result, turned, product, tilted, crossed, packed, fil_sem, cross_sem, send_sem):
    rows = 2 * GROUP
    groups = spectra.shape[0]

    def fetch(g):
        return pltpu.make_async_copy(fil.at[g], spectra.at[g], fil_sem.at[g])

    def put(g):
        return (pltpu.make_async_copy(crossed.at[g], cross.at[g], cross_sem.at[g]),
                pltpu.make_async_copy(packed.at[g], send.at[:, pl.ds(pl.multiple_of(g * rows, rows), rows), :], send_sem.at[g]))

    for g in range(groups):
        fetch(g).start()

    @pl.loop(0, groups)
    def _(g):
        fetch(g).wait()
        load_octets(got.at[:, pl.ds(pl.multiple_of(g * rows, rows), rows), :], stage)
        for c in range(GROUP):
            mix = stage[c // OCTET, pl.ds(c % OCTET, SIDE, stride=OCTET), :]
            wgt = stage[(c + GROUP) // OCTET, pl.ds((c + GROUP) % OCTET, SIDE, stride=OCTET), :]
            skip[g, c:c + 1, :] = jnp.sum(mix * wgt, axis=0, keepdims=True)
            keep(turned, c, turn_folded(fold_pair(join([mix, wgt], 1), True, fold, None), turn_re, turn_im), 1)
        for c in range(GROUP):
            both = rows_times(turned, c, spread, None, 1)
            mr, mi = both[:SIDE, :SIDE], both[:SIDE, SIDE:]
            wr, wi = both[SIDE:, :SIDE], both[SIDE:, SIDE:]
            fr, fi = spectra[g, c, :, :SIDE], spectra[g, c, :, SIDE:]
            crossed[g, c, :, :SIDE] = (wr * mr + wi * mi).astype(BF16)
            crossed[g, c, :, SIDE:] = (wi * mr - wr * mi).astype(BF16)
            keep(product, c, join([
                join([fr * mr - fi * mi, fr * mi + fi * mr], 1),
                join([fr * wr + fi * wi, fr * wi - fi * wr], 1),
            ], 0), 1)
        for c in range(GROUP):
            keep(tilted, c, turn_back(rows_times(product, c, gather, None, 1), turn_re, turn_im), 2)
        for c in range(GROUP):
            back = times_rows(unfold_hi, unfold_lo, tilted, c, 2)
            result[c // OCTET, pl.ds(c % OCTET, SIDE, stride=OCTET), :] = back[:, :SIDE]
            result[(c + GROUP) // OCTET, pl.ds((c + GROUP) % OCTET, SIDE, stride=OCTET), :] = back[:, SIDE:]
        store_octets(result, packed.at[g])
        for copy in put(g):
            copy.start()

    for g in range(groups):
        for copy in put(g):
            copy.wait()


def grad_kernel(scale, cross, turn_re, turn_im, gather_hi, gather_lo, unfold_hi, unfold_lo, out, stage, tilted):
    tr, ti = turn_re, turn_im
    pairs = cross.reshape(1, GROUP * SIDE, 2 * SIDE)
    for p in range(GROUP // 2):
        keep(tilted, p, turn_back(rows_times(pairs, p, gather_hi, gather_lo, 2), tr, ti), 3)
    for p in range(GROUP // 2):
        back = times_rows(unfold_hi, unfold_lo, tilted, p, 3) * scale
        for s in range(2):
            stage[pl.ds(2 * p + s, SIDE, stride=GROUP), :] = back[:, s * SIDE:(s + 1) * SIDE]
    for a in range(SIDE):
        out[:, a * SIDE:(a + 1) * SIDE] = stage[a * GROUP:(a + 1) * GROUP, :]


def held(signals):
    return pltpu.VMEM((2, signals * SIDE, 2 * SIDE), BF16)


def whole(array):
    return pl.BlockSpec(array.shape, lambda g: (0,) * array.ndim)


FAR = pl.BlockSpec(memory_space=pltpu.HBM)
NEAR = pl.BlockSpec(memory_space=pltpu.VMEM)


def granted(mib):
    return pltpu.CompilerParams(vmem_limit_bytes=mib * 1024 * 1024)


PARAMS = granted(60)


def cost(rows, moved):
    return pl.CostEstimate(flops=2 * rows * 256 * 256, bytes_accessed=moved, transcendentals=0)


def filter_spectra(filters, tab):
    channels, seq = filters.shape
    groups = channels // GROUP
    ops = [tab[k] for k in ("fold", "fold_hi", "turn_re", "turn_im", "spread_hi", "spread_lo")]
    return pl.pallas_call(
        filter_kernel,
        grid=(groups,),
        in_specs=[pl.BlockSpec((GROUP, seq), lambda g: (g, 0))] + [whole(o) for o in ops],
        out_specs=pl.BlockSpec((1, GROUP, SIDE, 2 * SIDE), lambda g: (g, 0, 0, 0)),
        out_shape=jax.ShapeDtypeStruct((groups, GROUP, SIDE, 2 * SIDE), F32),
        scratch_shapes=[pltpu.VMEM((SIDE * GROUP, SIDE), F32), held(GROUP)],
        compiler_params=PARAMS,
        cost_estimate=cost(channels * 5 * SIDE, 6 * channels * seq * 2),
        name="filter_spectra",
    )(filters, *ops)


def convolve(got, spec, tab, passes):
    groups = spec.shape[0]
    channels = groups * GROUP
    ops = [tab[k] for k in ("fold", "turn_re", "turn_im", "spread_one", "gather_one", "level_hi", "level_lo")]
    rows = 2 * GROUP
    return pl.pallas_call(
        signal_kernel,
        in_specs=[NEAR, FAR] + [NEAR] * len(ops),
        out_specs=[FAR, FAR, NEAR],
        out_shape=[pltpu.HBM((SIDE, 2 * channels, SIDE), BF16),
                   pltpu.HBM(spec.shape, BF16),
                   jax.ShapeDtypeStruct((groups, GROUP, SIDE), F32)],
        scratch_shapes=[pltpu.VMEM(spec.shape, F32)] + [pltpu.VMEM((rows // OCTET, SIDE * OCTET, SIDE), F32)] * 2 + [held(2 * GROUP)] * 3
        + [pltpu.VMEM(spec.shape, BF16), pltpu.VMEM((groups, SIDE, rows, SIDE), BF16)]
        + [pltpu.SemaphoreType.DMA((groups,))] * 3,
        compiler_params=granted(48),
        cost_estimate=cost(channels * 17 * SIDE, 12 * channels * SIDE * SIDE),
        name="convolve",
    )(got, spec, *ops)


def filter_gradient(cross, tab, scale):
    groups = cross.shape[0]
    channels = groups * GROUP
    ops = [tab[k] for k in ("turn_re", "turn_im", "gather_hi", "gather_lo", "unfold_hi", "unfold_lo")]
    return pl.pallas_call(
        functools.partial(grad_kernel, scale / tab["cross_gain"]),
        grid=(groups,),
        in_specs=[pl.BlockSpec((1, GROUP, SIDE, 2 * SIDE), lambda g: (g, 0, 0, 0))] + [whole(o) for o in ops],
        out_specs=pl.BlockSpec((GROUP, SIDE * SIDE), lambda g: (g, 0)),
        out_shape=jax.ShapeDtypeStruct((channels, SIDE * SIDE), F32),
        scratch_shapes=[pltpu.VMEM((SIDE * GROUP, SIDE), F32), held(GROUP)],
        compiler_params=PARAMS,
        cost_estimate=cost(channels * 5 * SIDE, 12 * channels * SIDE * SIDE),
        name="filter_gradient",
    )(cross, *ops)


PIECES = 4


def chunk(array, i):
    size = array.shape[0] // PIECES
    return array.at[pl.ds(i * size, size)]


def fetches(sources, stores, sems):
    return [[pltpu.make_async_copy(chunk(s, i), chunk(d, i), sems.at[j, i]) for j, (s, d) in enumerate(zip(sources, stores))]
            for i in range(PIECES)]


def products_kernel(query, key_in, value_in, cotangent, out, q, k, v, c, both, in_sem, out_sem):
    loads = fetches((query, key_in, value_in, cotangent), (q, k, v, c), in_sem)
    stores = [s[0] for s in fetches((both,), (out,), out_sem)]
    for group in loads:
        for copy in group:
            copy.start()
    for i in range(PIECES):
        for copy in loads[i]:
            copy.wait()
        qi, ki, vi, ci = [chunk(x, i)[...].astype(F32) for x in (q, k, v, c)]
        pair = jnp.stack([x.reshape(-1, GROUP, SIDE) for x in (ki * vi, ci * qi)], axis=1)
        chunk(both, i)[...] = pair.reshape(chunk(both, i).shape).astype(BF16)
        stores[i].start()
    for copy in stores:
        copy.wait()


def products(query, key_in, value_in, cotangent, own):
    channels = query.shape[0]
    sent = (channels // own, 2 * own, SIDE)
    return pl.pallas_call(
        products_kernel,
        in_specs=[FAR] * 4,
        out_specs=FAR,
        out_shape=jax.ShapeDtypeStruct(sent, BF16),
        scratch_shapes=[pltpu.VMEM(query.shape, BF16)] * 4 + [pltpu.VMEM(sent, BF16)]
        + [pltpu.SemaphoreType.DMA((4, PIECES)), pltpu.SemaphoreType.DMA((1, PIECES))],
        compiler_params=PARAMS,
        cost_estimate=pl.CostEstimate(flops=2 * channels * SIDE, bytes_accessed=12 * channels * SIDE, transcendentals=0),
        name="products",
    )(query, key_in, value_in, cotangent)


def finish_kernel(query, key_in, value_in, cotangent, got, gain, output, grad_query, grad_key, grad_value,
                  k, v, c, spread, out_a, out_b, out_c, out_d, in_sem, out_sem):
    results = (out_a, out_b, out_c, out_d)
    loads = fetches((key_in, value_in, cotangent), (k, v, c), in_sem)
    stores = fetches(results, (output, grad_query, grad_key, grad_value), out_sem)
    for group in loads:
        for copy in group:
            copy.start()
    for i in range(gain.shape[0]):
        spread[i * SIDE:(i + 1) * SIDE, :] = jnp.broadcast_to(gain[i:i + 1, :], (SIDE, SIDE)).T
    for i in range(PIECES):
        for copy in loads[i]:
            copy.wait()
        qi, ki, vi, ci, pair = [chunk(x, i)[...].astype(F32) for x in (query, k, v, c, got)]
        pair = pair.reshape(-1, 2, GROUP, SIDE)
        conv, back = pair[:, 0].reshape(qi.shape), pair[:, 1].reshape(qi.shape)
        g = chunk(spread, i)[...]
        inner = conv + g * (ki * vi).astype(BF16).astype(F32)
        dmixed = back + g * (ci * qi).astype(BF16).astype(F32)
        for store, value in zip(results, (qi * inner, ci * inner, dmixed * vi, dmixed * ki)):
            chunk(store, i)[...] = value.astype(BF16)
        for copy in stores[i]:
            copy.start()
    for group in stores:
        for copy in group:
            copy.wait()


def finish(query, key_in, value_in, cotangent, got, gain):
    channels = query.shape[0]
    return pl.pallas_call(
        finish_kernel,
        in_specs=[NEAR] + [FAR] * 3 + [NEAR] * 2,
        out_specs=[FAR] * 4,
        out_shape=[jax.ShapeDtypeStruct(query.shape, BF16)] * 4,
        scratch_shapes=[pltpu.VMEM(query.shape, BF16)] * 3 + [pltpu.VMEM(query.shape, F32)]
        + [pltpu.VMEM(query.shape, BF16)] * 4
        + [pltpu.SemaphoreType.DMA((3, PIECES)), pltpu.SemaphoreType.DMA((4, PIECES))],
        compiler_params=granted(48),
        cost_estimate=pl.CostEstimate(flops=10 * channels * SIDE, bytes_accessed=20 * channels * SIDE, transcendentals=0),
        name="finish",
    )(query, key_in, value_in, cotangent, got, gain)


def far(array):
    return pltpu.with_memory_space_constraint(array, pltpu.HBM)


def exchange(blocks):
    return lax.all_to_all(blocks, ("node", "local"), split_axis=0, concat_axis=0, tiled=True)


def local(query, key_in, value_in, filters, skip_gain, cotangent):
    tab = tables()
    scale = float(filters.shape[1]) ** -0.5
    got = exchange(products(query, key_in, value_in, cotangent, filters.shape[0]))
    spec = filter_spectra(filters, tab)
    gain = skip_gain.reshape(-1, SIDE)
    send, cross, skip = convolve(got, spec, tab, (1, 1, 2))
    back = exchange(send)
    grad_filters = filter_gradient(cross, tab, scale)
    grad_skip = jnp.sum(skip.reshape(-1, SIDE), axis=1) * scale
    return (*finish(query, far(key_in), far(value_in), far(cotangent), back, gain), grad_filters, grad_skip)


def solution(mesh):
    tokens = P(None, ("node", "local"))
    return jax.shard_map(
        local,
        mesh=mesh,
        in_specs=(tokens, tokens, tokens, P(("node", "local"), None), P(), tokens),
        out_specs=(tokens, tokens, tokens, tokens, P(("node", "local"), None), P(("node", "local"))),
        check_vma=False,
    )
```

```python
import functools

import jax
import jax.numpy as jnp
import numpy as np
from jax import lax
from jax.experimental import pallas as pl
from jax.experimental.pallas import tpu as pltpu
from jax.sharding import PartitionSpec as P

F32 = jnp.float32
BF16 = jnp.bfloat16
SIDE = 128
TILT = 1.62305
GROUP = 8
OCTET = 8


def two_terms(values):
    high = np.asarray(values, np.float32).astype(BF16)
    low = (values - high.astype(np.float64)).astype(np.float32).astype(BF16)
    return high, low


def one_term(values):
    high = (values * TILT).astype(np.float32).astype(BF16)
    wide = high.astype(np.float64)
    return high, float((wide * values).sum() / (values * values).sum())


def tables():
    index = np.arange(SIDE, dtype=np.float64)
    psi = 2.0 * np.pi * index[:, None] * (index[None, :] + 0.25) / SIDE
    phi = 2.0 * np.pi * (index[:, None] + 0.25) * index[None, :] / (SIDE * SIDE)
    theta = 2.0 * np.pi * ((index[:, None] * index[None, :]) % SIDE) / SIDE
    cos_t, sin_t = np.cos(theta), np.sin(theta)
    fold = np.concatenate([np.cos(psi).T, -np.sin(psi).T], axis=0)
    fold_hi, fold_lo = two_terms(fold)
    spread_hi, spread_lo = two_terms(np.block([[cos_t, -sin_t], [sin_t, cos_t]]))
    gather_hi, gather_lo = two_terms(np.block([[cos_t, sin_t], [-sin_t, cos_t]]) / SIDE)
    unfold = np.concatenate([np.cos(psi), -np.sin(psi)], axis=1) / SIDE
    unfold_hi, unfold_lo = two_terms(unfold)
    spread_one, spread_gain = one_term(np.block([[cos_t, -sin_t], [sin_t, cos_t]]))
    gather_one, gather_gain = one_term(np.block([[cos_t, sin_t], [-sin_t, cos_t]]) / SIDE)
    level_hi, level_lo = two_terms(unfold / (spread_gain * gather_gain))
    return dict(
        fold=np.concatenate([fold_hi, fold_lo], axis=1),
        fold_hi=fold_hi,
        turn_re=np.cos(phi).astype(np.float32),
        turn_im=np.sin(phi).astype(np.float32),
        spread_hi=spread_hi, spread_lo=spread_lo,
        gather_hi=gather_hi, gather_lo=gather_lo,
        unfold_hi=unfold_hi, unfold_lo=unfold_lo,
        spread_one=spread_one, gather_one=gather_one,
        level_hi=level_hi, level_lo=level_lo, cross_gain=spread_gain**2,
    )


def dot(lhs, rhs):
    return jnp.dot(lhs, rhs, preferred_element_type=F32)


def join(parts, axis):
    return jnp.concatenate(parts, axis=axis)


def fold_pair(pair, exact, fold, fold_hi):
    high = pair.astype(BF16)
    folded = dot(fold[...], join([high, high], 0))
    if not exact:
        folded = folded + dot(fold_hi[...], (pair - high.astype(F32)).astype(BF16))
    return folded


def turn_folded(folded, cos_ref, sin_ref):
    turn_re, turn_im = cos_ref[...], sin_ref[...]
    rows = []
    for s in range(2):
        re, im = folded[:SIDE, s * SIDE:(s + 1) * SIDE], folded[SIDE:, s * SIDE:(s + 1) * SIDE]
        rows.append(join([re * turn_re + im * turn_im, im * turn_re - re * turn_im], 1))
    return join(rows, 0)


def turn_back(part, cos_ref, sin_ref):
    turn_re, turn_im = cos_ref[...], sin_ref[...]
    cols = []
    for s in range(2):
        re, im = part[s * SIDE:(s + 1) * SIDE, :SIDE], part[s * SIDE:(s + 1) * SIDE, SIDE:]
        cols.append(join([re * turn_re - im * turn_im, im * turn_re + re * turn_im], 0))
    return join(cols, 1)


def keep(store, c, values, passes):
    rows = pl.ds(c * 2 * SIDE, 2 * SIDE)
    high = values.astype(BF16)
    store[0, rows, :] = high
    if passes % 2 == 1 and passes > 1:
        store[1, rows, :] = (values - high.astype(F32)).astype(BF16)


def rows_times(store, c, hi, lo, passes):
    rows = pl.ds(c * 2 * SIDE, 2 * SIDE)
    high = store[0, rows, :]
    lhs, rhs = [high], [hi[...]]
    if passes >= 2:
        lhs, rhs = lhs + [high], rhs + [lo[...]]
    if passes >= 3:
        lhs, rhs = lhs + [store[1, rows, :]], rhs + [hi[...]]
    return dot(join(lhs, 1), join(rhs, 0))


def times_rows(hi, lo, store, c, passes):
    rows = pl.ds(c * 2 * SIDE, 2 * SIDE)
    high = store[0, rows, :]
    if passes == 2:
        both = dot(join([hi[...], lo[...]], 0), high)
        return both[:SIDE] + both[SIDE:]
    lhs, rhs = [hi[...]], [high]
    if passes >= 2:
        lhs, rhs = lhs + [lo[...]], rhs + [high]
    if passes >= 3:
        lhs, rhs = lhs + [hi[...]], rhs + [store[1, rows, :]]
    return dot(join(lhs, 1), join(rhs, 0))


def filter_kernel(fil, fold, fold_hi, turn_re, turn_im, spread_hi, spread_lo, spec, stage, turned):
    for a in range(SIDE):
        stage[a * GROUP:(a + 1) * GROUP, :] = fil[:, a * SIDE:(a + 1) * SIDE]
    tr, ti = turn_re, turn_im
    for p in range(GROUP // 2):
        pair = join([stage[pl.ds(2 * p + s, SIDE, stride=GROUP), :] for s in range(2)], 1)
        keep(turned, p, turn_folded(fold_pair(pair, False, fold, fold_hi), tr, ti), 3)
    for p in range(GROUP // 2):
        out = rows_times(turned, p, spread_hi, spread_lo, 3)
        spec[0, 2 * p] = out[:SIDE]
        spec[0, 2 * p + 1] = out[SIDE:]


def load_octets(source, stage):
    for o in range(stage.shape[0]):
        pair = source[:, o // 2 * 2 * OCTET:(o // 2 + 1) * 2 * OCTET, :].astype(F32)
        stage[o] = pair[:, o % 2 * OCTET:(o % 2 + 1) * OCTET].reshape(SIDE * OCTET, SIDE)


def store_octets(result, target):
    for o in range(0, result.shape[0], 2):
        pair = join([result[o + i].reshape(SIDE, OCTET, SIDE) for i in range(2)], 1)
        target[:, o * OCTET:(o + 2) * OCTET, :] = pair.astype(BF16)


def signal_kernel(got, fil, fold, turn_re, turn_im, spread, gather, unfold_hi, unfold_lo,
                  send, cross, skip, spectra, stage, result, turned, product, tilted, crossed, packed, fil_sem, cross_sem, send_sem):
    rows = 2 * GROUP
    groups = spectra.shape[0]

    def fetch(g):
        return pltpu.make_async_copy(fil.at[g], spectra.at[g], fil_sem.at[g])

    def put(g):
        return (pltpu.make_async_copy(crossed.at[g], cross.at[g], cross_sem.at[g]),
                pltpu.make_async_copy(packed.at[g], send.at[:, pl.ds(g * rows, rows), :], send_sem.at[g]))

    for g in range(groups):
        fetch(g).start()

    for g in range(groups):
        if g > 0:
            fetch(g).wait()
        load_octets(got.at[:, pl.ds(g * rows, rows), :], stage)
        for c in range(GROUP):
            mix = stage[c // OCTET, pl.ds(c % OCTET, SIDE, stride=OCTET), :]
            wgt = stage[(c + GROUP) // OCTET, pl.ds((c + GROUP) % OCTET, SIDE, stride=OCTET), :]
            skip[g, c:c + 1, :] = jnp.sum(mix * wgt, axis=0, keepdims=True)
            keep(turned, c, turn_folded(fold_pair(join([mix, wgt], 1), True, fold, None), turn_re, turn_im), 1)
        if g == 0:
            fetch(g).wait()
        for c in range(GROUP):
            both = rows_times(turned, c, spread, None, 1)
            mr, mi = both[:SIDE, :SIDE], both[:SIDE, SIDE:]
            wr, wi = both[SIDE:, :SIDE], both[SIDE:, SIDE:]
            fr, fi = spectra[g, c, :, :SIDE], spectra[g, c, :, SIDE:]
            crossed[g, c, :, :SIDE] = (wr * mr + wi * mi).astype(BF16)
            crossed[g, c, :, SIDE:] = (wi * mr - wr * mi).astype(BF16)
            keep(product, c, join([
                join([fr * mr - fi * mi, fr * mi + fi * mr], 1),
                join([fr * wr + fi * wi, fr * wi - fi * wr], 1),
            ], 0), 1)
        cross_out, send_out = put(g)
        if g == groups - 1:
            cross_out.start()
        for c in range(GROUP):
            keep(tilted, c, turn_back(rows_times(product, c, gather, None, 1), turn_re, turn_im), 2)
        for c in range(GROUP):
            back = times_rows(unfold_hi, unfold_lo, tilted, c, 2)
            result[c // OCTET, pl.ds(c % OCTET, SIDE, stride=OCTET), :] = back[:, :SIDE]
            result[(c + GROUP) // OCTET, pl.ds((c + GROUP) % OCTET, SIDE, stride=OCTET), :] = back[:, SIDE:]
        store_octets(result, packed.at[g])
        if g < groups - 1:
            cross_out.start()
        send_out.start()

    for g in range(groups):
        for copy in put(g):
            copy.wait()


def grad_kernel(scale, cross, turn_re, turn_im, gather_hi, gather_lo, unfold_hi, unfold_lo, out, stage, tilted):
    tr, ti = turn_re, turn_im
    pairs = cross.reshape(1, GROUP * SIDE, 2 * SIDE)
    for p in range(GROUP // 2):
        keep(tilted, p, turn_back(rows_times(pairs, p, gather_hi, gather_lo, 2), tr, ti), 3)
    for p in range(GROUP // 2):
        back = times_rows(unfold_hi, unfold_lo, tilted, p, 3) * scale
        for s in range(2):
            stage[pl.ds(2 * p + s, SIDE, stride=GROUP), :] = back[:, s * SIDE:(s + 1) * SIDE]
    for a in range(SIDE):
        out[:, a * SIDE:(a + 1) * SIDE] = stage[a * GROUP:(a + 1) * GROUP, :]


def held(signals):
    return pltpu.VMEM((2, signals * SIDE, 2 * SIDE), BF16)


def whole(array):
    return pl.BlockSpec(array.shape, lambda g: (0,) * array.ndim)


FAR = pl.BlockSpec(memory_space=pltpu.HBM)
NEAR = pl.BlockSpec(memory_space=pltpu.VMEM)


def granted(mib):
    return pltpu.CompilerParams(vmem_limit_bytes=mib * 1024 * 1024)


PARAMS = granted(60)


def cost(rows, moved):
    return pl.CostEstimate(flops=2 * rows * 256 * 256, bytes_accessed=moved, transcendentals=0)


def filter_spectra(filters, tab):
    channels, seq = filters.shape
    groups = channels // GROUP
    ops = [tab[k] for k in ("fold", "fold_hi", "turn_re", "turn_im", "spread_hi", "spread_lo")]
    return pl.pallas_call(
        filter_kernel,
        grid=(groups,),
        in_specs=[pl.BlockSpec((GROUP, seq), lambda g: (g, 0))] + [whole(o) for o in ops],
        out_specs=pl.BlockSpec((1, GROUP, SIDE, 2 * SIDE), lambda g: (g, 0, 0, 0)),
        out_shape=jax.ShapeDtypeStruct((groups, GROUP, SIDE, 2 * SIDE), F32),
        scratch_shapes=[pltpu.VMEM((SIDE * GROUP, SIDE), F32), held(GROUP)],
        compiler_params=PARAMS,
        cost_estimate=cost(channels * 5 * SIDE, 6 * channels * seq * 2),
        name="filter_spectra",
    )(filters, *ops)


def convolve(got, spec, tab, passes):
    groups = spec.shape[0]
    channels = groups * GROUP
    ops = [tab[k] for k in ("fold", "turn_re", "turn_im", "spread_one", "gather_one", "level_hi", "level_lo")]
    rows = 2 * GROUP
    return pl.pallas_call(
        signal_kernel,
        in_specs=[NEAR, FAR] + [NEAR] * len(ops),
        out_specs=[FAR, FAR, NEAR],
        out_shape=[pltpu.HBM((SIDE, 2 * channels, SIDE), BF16),
                   pltpu.HBM(spec.shape, BF16),
                   jax.ShapeDtypeStruct((groups, GROUP, SIDE), F32)],
        scratch_shapes=[pltpu.VMEM(spec.shape, F32)] + [pltpu.VMEM((rows // OCTET, SIDE * OCTET, SIDE), F32)] * 2 + [held(2 * GROUP)] * 3
        + [pltpu.VMEM(spec.shape, BF16), pltpu.VMEM((groups, SIDE, rows, SIDE), BF16)]
        + [pltpu.SemaphoreType.DMA((groups,))] * 3,
        compiler_params=granted(48),
        cost_estimate=cost(channels * 17 * SIDE, 12 * channels * SIDE * SIDE),
        name="convolve",
    )(got, spec, *ops)


def filter_gradient(cross, tab, scale):
    groups = cross.shape[0]
    channels = groups * GROUP
    ops = [tab[k] for k in ("turn_re", "turn_im", "gather_hi", "gather_lo", "unfold_hi", "unfold_lo")]
    return pl.pallas_call(
        functools.partial(grad_kernel, scale / tab["cross_gain"]),
        grid=(groups,),
        in_specs=[pl.BlockSpec((1, GROUP, SIDE, 2 * SIDE), lambda g: (g, 0, 0, 0))] + [whole(o) for o in ops],
        out_specs=pl.BlockSpec((GROUP, SIDE * SIDE), lambda g: (g, 0)),
        out_shape=jax.ShapeDtypeStruct((channels, SIDE * SIDE), F32),
        scratch_shapes=[pltpu.VMEM((SIDE * GROUP, SIDE), F32), held(GROUP)],
        compiler_params=PARAMS,
        cost_estimate=cost(channels * 5 * SIDE, 12 * channels * SIDE * SIDE),
        name="filter_gradient",
    )(cross, *ops)


PIECES = 4


def chunk(array, i):
    size = array.shape[0] // PIECES
    return array.at[pl.ds(i * size, size)]


def fetches(sources, stores, sems):
    return [[pltpu.make_async_copy(chunk(s, i), chunk(d, i), sems.at[j, i]) for j, (s, d) in enumerate(zip(sources, stores))]
            for i in range(PIECES)]


def products_kernel(query, key_in, value_in, cotangent, out, q, k, v, c, both, in_sem, out_sem):
    loads = fetches((query, key_in, value_in, cotangent), (q, k, v, c), in_sem)
    stores = [s[0] for s in fetches((both,), (out,), out_sem)]
    for group in loads:
        for copy in group:
            copy.start()
    for i in range(PIECES):
        for copy in loads[i]:
            copy.wait()
        qi, ki, vi, ci = [chunk(x, i)[...].astype(F32) for x in (q, k, v, c)]
        pair = jnp.stack([x.reshape(-1, GROUP, SIDE) for x in (ki * vi, ci * qi)], axis=1)
        chunk(both, i)[...] = pair.reshape(chunk(both, i).shape).astype(BF16)
        stores[i].start()
    for copy in stores:
        copy.wait()


def products(query, key_in, value_in, cotangent, own):
    channels = query.shape[0]
    sent = (channels // own, 2 * own, SIDE)
    return pl.pallas_call(
        products_kernel,
        in_specs=[FAR] * 4,
        out_specs=FAR,
        out_shape=jax.ShapeDtypeStruct(sent, BF16),
        scratch_shapes=[pltpu.VMEM(query.shape, BF16)] * 4 + [pltpu.VMEM(sent, BF16)]
        + [pltpu.SemaphoreType.DMA((4, PIECES)), pltpu.SemaphoreType.DMA((1, PIECES))],
        compiler_params=PARAMS,
        cost_estimate=pl.CostEstimate(flops=2 * channels * SIDE, bytes_accessed=12 * channels * SIDE, transcendentals=0),
        name="products",
    )(query, key_in, value_in, cotangent)


def finish_kernel(query, key_in, value_in, cotangent, got, gain, output, grad_query, grad_key, grad_value,
                  k, v, c, spread, out_a, out_b, out_c, out_d, in_sem, out_sem):
    results = (out_a, out_b, out_c, out_d)
    loads = fetches((key_in, value_in, cotangent), (k, v, c), in_sem)
    stores = fetches(results, (output, grad_query, grad_key, grad_value), out_sem)
    for group in loads:
        for copy in group:
            copy.start()
    for i in range(gain.shape[0]):
        spread[i * SIDE:(i + 1) * SIDE, :] = jnp.broadcast_to(gain[i:i + 1, :], (SIDE, SIDE)).T
    for i in range(PIECES):
        for copy in loads[i]:
            copy.wait()
        qi, ki, vi, ci, pair = [chunk(x, i)[...].astype(F32) for x in (query, k, v, c, got)]
        pair = pair.reshape(-1, 2, GROUP, SIDE)
        conv, back = pair[:, 0].reshape(qi.shape), pair[:, 1].reshape(qi.shape)
        g = chunk(spread, i)[...]
        inner = conv + g * (ki * vi).astype(BF16).astype(F32)
        dmixed = back + g * (ci * qi).astype(BF16).astype(F32)
        for store, value in zip(results, (qi * inner, ci * inner, dmixed * vi, dmixed * ki)):
            chunk(store, i)[...] = value.astype(BF16)
        for copy in stores[i]:
            copy.start()
    for group in stores:
        for copy in group:
            copy.wait()


def finish(query, key_in, value_in, cotangent, got, gain):
    channels = query.shape[0]
    return pl.pallas_call(
        finish_kernel,
        in_specs=[NEAR] + [FAR] * 3 + [NEAR] * 2,
        out_specs=[FAR] * 4,
        out_shape=[jax.ShapeDtypeStruct(query.shape, BF16)] * 4,
        scratch_shapes=[pltpu.VMEM(query.shape, BF16)] * 3 + [pltpu.VMEM(query.shape, F32)]
        + [pltpu.VMEM(query.shape, BF16)] * 4
        + [pltpu.SemaphoreType.DMA((3, PIECES)), pltpu.SemaphoreType.DMA((4, PIECES))],
        compiler_params=granted(48),
        cost_estimate=pl.CostEstimate(flops=10 * channels * SIDE, bytes_accessed=20 * channels * SIDE, transcendentals=0),
        name="finish",
    )(query, key_in, value_in, cotangent, got, gain)


def far(array):
    return pltpu.with_memory_space_constraint(array, pltpu.HBM)


def exchange(blocks):
    return lax.all_to_all(blocks, ("node", "local"), split_axis=0, concat_axis=0, tiled=True)


def local(query, key_in, value_in, filters, skip_gain, cotangent):
    tab = tables()
    scale = float(filters.shape[1]) ** -0.5
    got = exchange(products(query, key_in, value_in, cotangent, filters.shape[0]))
    spec = filter_spectra(filters, tab)
    gain = skip_gain.reshape(-1, SIDE)
    send, cross, skip = convolve(got, spec, tab, (1, 1, 2))
    back = exchange(send)
    grad_filters = filter_gradient(cross, tab, scale)
    grad_skip = jnp.sum(skip.reshape(-1, SIDE), axis=1) * scale
    return (*finish(query, far(key_in), far(value_in), far(cotangent), back, gain), grad_filters, grad_skip)


def solution(mesh):
    tokens = P(None, ("node", "local"))
    return jax.shard_map(
        local,
        mesh=mesh,
        in_specs=(tokens, tokens, tokens, P(("node", "local"), None), P(), tokens),
        out_specs=(tokens, tokens, tokens, tokens, P(("node", "local"), None), P(("node", "local"))),
        check_vma=False,
    )
```

```python
import functools

import jax
import jax.numpy as jnp
import numpy as np
from jax import lax
from jax.experimental import pallas as pl
from jax.experimental.pallas import tpu as pltpu
from jax.sharding import PartitionSpec as P

F32 = jnp.float32
BF16 = jnp.bfloat16
SIDE = 128
TILT = 1.62305
GROUP = 8
OCTET = 8


def two_terms(values):
    high = np.asarray(values, np.float32).astype(BF16)
    low = (values - high.astype(np.float64)).astype(np.float32).astype(BF16)
    return high, low


def one_term(values):
    high = (values * TILT).astype(np.float32).astype(BF16)
    wide = high.astype(np.float64)
    return high, float((wide * values).sum() / (values * values).sum())


def tables():
    index = np.arange(SIDE, dtype=np.float64)
    psi = 2.0 * np.pi * index[:, None] * (index[None, :] + 0.25) / SIDE
    phi = 2.0 * np.pi * (index[:, None] + 0.25) * index[None, :] / (SIDE * SIDE)
    theta = 2.0 * np.pi * ((index[:, None] * index[None, :]) % SIDE) / SIDE
    cos_t, sin_t = np.cos(theta), np.sin(theta)
    fold = np.concatenate([np.cos(psi).T, -np.sin(psi).T], axis=0)
    fold_hi, fold_lo = two_terms(fold)
    spread_hi, spread_lo = two_terms(np.block([[cos_t, -sin_t], [sin_t, cos_t]]))
    gather_hi, gather_lo = two_terms(np.block([[cos_t, sin_t], [-sin_t, cos_t]]) / SIDE)
    unfold = np.concatenate([np.cos(psi), -np.sin(psi)], axis=1) / SIDE
    unfold_hi, unfold_lo = two_terms(unfold)
    spread_one, spread_gain = one_term(np.block([[cos_t, -sin_t], [sin_t, cos_t]]))
    gather_one, gather_gain = one_term(np.block([[cos_t, sin_t], [-sin_t, cos_t]]) / SIDE)
    level_hi, level_lo = two_terms(unfold / (spread_gain * gather_gain))
    return dict(
        fold=np.concatenate([fold_hi, fold_lo], axis=1),
        fold_hi=fold_hi,
        turn_re=np.cos(phi).astype(np.float32),
        turn_im=np.sin(phi).astype(np.float32),
        spread_hi=spread_hi, spread_lo=spread_lo,
        gather_hi=gather_hi, gather_lo=gather_lo,
        unfold_hi=unfold_hi, unfold_lo=unfold_lo,
        spread_one=spread_one, gather_one=gather_one,
        level_hi=level_hi, level_lo=level_lo, cross_gain=spread_gain**2,
    )


def dot(lhs, rhs):
    return jnp.dot(lhs, rhs, preferred_element_type=F32)


def join(parts, axis):
    return jnp.concatenate(parts, axis=axis)


def fold_pair(pair, exact, fold, fold_hi):
    high = pair.astype(BF16)
    folded = dot(fold[...], join([high, high], 0))
    if not exact:
        folded = folded + dot(fold_hi[...], (pair - high.astype(F32)).astype(BF16))
    return folded


def turn_folded(folded, cos_ref, sin_ref):
    turn_re, turn_im = cos_ref[...], sin_ref[...]
    rows = []
    for s in range(2):
        re, im = folded[:SIDE, s * SIDE:(s + 1) * SIDE], folded[SIDE:, s * SIDE:(s + 1) * SIDE]
        rows.append(join([re * turn_re + im * turn_im, im * turn_re - re * turn_im], 1))
    return join(rows, 0)


def turn_back(part, cos_ref, sin_ref):
    turn_re, turn_im = cos_ref[...], sin_ref[...]
    cols = []
    for s in range(2):
        re, im = part[s * SIDE:(s + 1) * SIDE, :SIDE], part[s * SIDE:(s + 1) * SIDE, SIDE:]
        cols.append(join([re * turn_re - im * turn_im, im * turn_re + re * turn_im], 0))
    return join(cols, 1)


def keep(store, c, values, passes):
    rows = pl.ds(c * 2 * SIDE, 2 * SIDE)
    high = values.astype(BF16)
    store[0, rows, :] = high
    if passes % 2 == 1 and passes > 1:
        store[1, rows, :] = (values - high.astype(F32)).astype(BF16)


def rows_times(store, c, hi, lo, passes):
    rows = pl.ds(c * 2 * SIDE, 2 * SIDE)
    high = store[0, rows, :]
    lhs, rhs = [high], [hi[...]]
    if passes >= 2:
        lhs, rhs = lhs + [high], rhs + [lo[...]]
    if passes >= 3:
        lhs, rhs = lhs + [store[1, rows, :]], rhs + [hi[...]]
    return dot(join(lhs, 1), join(rhs, 0))


def times_rows(hi, lo, store, c, passes):
    rows = pl.ds(c * 2 * SIDE, 2 * SIDE)
    high = store[0, rows, :]
    if passes == 2:
        both = dot(join([hi[...], lo[...]], 0), high)
        return both[:SIDE] + both[SIDE:]
    lhs, rhs = [hi[...]], [high]
    if passes >= 2:
        lhs, rhs = lhs + [lo[...]], rhs + [high]
    if passes >= 3:
        lhs, rhs = lhs + [hi[...]], rhs + [store[1, rows, :]]
    return dot(join(lhs, 1), join(rhs, 0))


def filter_kernel(fil, fold, fold_hi, turn_re, turn_im, spread_hi, spread_lo, spec, stage, turned):
    for a in range(SIDE):
        stage[a * GROUP:(a + 1) * GROUP, :] = fil[:, a * SIDE:(a + 1) * SIDE]
    tr, ti = turn_re, turn_im
    for p in range(GROUP // 2):
        pair = join([stage[pl.ds(2 * p + s, SIDE, stride=GROUP), :] for s in range(2)], 1)
        keep(turned, p, turn_folded(fold_pair(pair, False, fold, fold_hi), tr, ti), 3)
    for p in range(GROUP // 2):
        out = rows_times(turned, p, spread_hi, spread_lo, 3)
        spec[0, 2 * p] = out[:SIDE]
        spec[0, 2 * p + 1] = out[SIDE:]


def load_octets(source, stage):
    for o in range(stage.shape[0]):
        pair = source[:, o // 2 * 2 * OCTET:(o // 2 + 1) * 2 * OCTET, :].astype(F32)
        stage[o] = pair[:, o % 2 * OCTET:(o % 2 + 1) * OCTET].reshape(SIDE * OCTET, SIDE)


def store_octets(result, target):
    for o in range(0, result.shape[0], 2):
        pair = join([result[o + i].reshape(SIDE, OCTET, SIDE) for i in range(2)], 1)
        target[:, o * OCTET:(o + 2) * OCTET, :] = pair.astype(BF16)


def signal_kernel(got, fil, fold, turn_re, turn_im, spread, gather, unfold_hi, unfold_lo,
                  send, cross, skip, spectra, stage, result, turned, product, tilted, crossed, packed, fil_sem, cross_sem, send_sem):
    rows = 2 * GROUP
    groups = spectra.shape[0]

    def fetch(g):
        return pltpu.make_async_copy(fil.at[g], spectra.at[g], fil_sem.at[g])

    def put(g):
        return (pltpu.make_async_copy(crossed.at[g], cross.at[g], cross_sem.at[g]),
                pltpu.make_async_copy(packed.at[g], send.at[:, pl.ds(g * rows, rows), :], send_sem.at[g]))

    for g in range(groups):
        fetch(g).start()

    for g in range(groups):
        if g > 0:
            fetch(g).wait()
        load_octets(got.at[:, pl.ds(g * rows, rows), :], stage)
        for c in range(GROUP):
            mix = stage[c // OCTET, pl.ds(c % OCTET, SIDE, stride=OCTET), :]
            wgt = stage[(c + GROUP) // OCTET, pl.ds((c + GROUP) % OCTET, SIDE, stride=OCTET), :]
            skip[g, c:c + 1, :] = jnp.sum(mix * wgt, axis=0, keepdims=True)
            keep(turned, c, turn_folded(fold_pair(join([mix, wgt], 1), True, fold, None), turn_re, turn_im), 1)
        if g == 0:
            fetch(g).wait()
        for c in range(GROUP):
            both = rows_times(turned, c, spread, None, 1)
            mr, mi = both[:SIDE, :SIDE], both[:SIDE, SIDE:]
            wr, wi = both[SIDE:, :SIDE], both[SIDE:, SIDE:]
            fr, fi = spectra[g, c, :, :SIDE], spectra[g, c, :, SIDE:]
            crossed[g, c, :, :SIDE] = (wr * mr + wi * mi).astype(BF16)
            crossed[g, c, :, SIDE:] = (wi * mr - wr * mi).astype(BF16)
            keep(product, c, join([
                join([fr * mr - fi * mi, fr * mi + fi * mr], 1),
                join([fr * wr + fi * wi, fr * wi - fi * wr], 1),
            ], 0), 1)
        cross_out, send_out = put(g)
        if g == groups - 1:
            cross_out.start()
        for c in range(GROUP):
            keep(tilted, c, turn_back(rows_times(product, c, gather, None, 1), turn_re, turn_im), 2)
        for c in range(GROUP):
            back = times_rows(unfold_hi, unfold_lo, tilted, c, 2)
            result[c // OCTET, pl.ds(c % OCTET, SIDE, stride=OCTET), :] = back[:, :SIDE]
            result[(c + GROUP) // OCTET, pl.ds((c + GROUP) % OCTET, SIDE, stride=OCTET), :] = back[:, SIDE:]
        store_octets(result, packed.at[g])
        if g < groups - 1:
            cross_out.start()
        send_out.start()

    for g in range(groups):
        for copy in put(g):
            copy.wait()


def grad_kernel(scale, cross, turn_re, turn_im, gather_hi, gather_lo, unfold_hi, unfold_lo, out, stage, tilted):
    tr, ti = turn_re, turn_im
    pairs = cross.reshape(1, GROUP * SIDE, 2 * SIDE)
    for p in range(GROUP // 2):
        keep(tilted, p, turn_back(rows_times(pairs, p, gather_hi, gather_lo, 2), tr, ti), 3)
    for p in range(GROUP // 2):
        back = times_rows(unfold_hi, unfold_lo, tilted, p, 3) * scale
        for s in range(2):
            stage[pl.ds(2 * p + s, SIDE, stride=GROUP), :] = back[:, s * SIDE:(s + 1) * SIDE]
    for a in range(SIDE):
        out[:, a * SIDE:(a + 1) * SIDE] = stage[a * GROUP:(a + 1) * GROUP, :]


def held(signals):
    return pltpu.VMEM((2, signals * SIDE, 2 * SIDE), BF16)


def whole(array):
    return pl.BlockSpec(array.shape, lambda g: (0,) * array.ndim)


FAR = pl.BlockSpec(memory_space=pltpu.HBM)
NEAR = pl.BlockSpec(memory_space=pltpu.VMEM)


def granted(mib):
    return pltpu.CompilerParams(vmem_limit_bytes=mib * 1024 * 1024)


PARAMS = granted(60)


def cost(rows, moved):
    return pl.CostEstimate(flops=2 * rows * 256 * 256, bytes_accessed=moved, transcendentals=0)


def filter_spectra(filters, tab):
    channels, seq = filters.shape
    groups = channels // GROUP
    ops = [tab[k] for k in ("fold", "fold_hi", "turn_re", "turn_im", "spread_hi", "spread_lo")]
    return pl.pallas_call(
        filter_kernel,
        grid=(groups,),
        in_specs=[pl.BlockSpec((GROUP, seq), lambda g: (g, 0))] + [whole(o) for o in ops],
        out_specs=pl.BlockSpec((1, GROUP, SIDE, 2 * SIDE), lambda g: (g, 0, 0, 0)),
        out_shape=jax.ShapeDtypeStruct((groups, GROUP, SIDE, 2 * SIDE), F32),
        scratch_shapes=[pltpu.VMEM((SIDE * GROUP, SIDE), F32), held(GROUP)],
        compiler_params=PARAMS,
        cost_estimate=cost(channels * 5 * SIDE, 6 * channels * seq * 2),
        name="filter_spectra",
    )(filters, *ops)


def convolve(got, spec, tab, passes):
    groups = spec.shape[0]
    channels = groups * GROUP
    ops = [tab[k] for k in ("fold", "turn_re", "turn_im", "spread_one", "gather_one", "level_hi", "level_lo")]
    rows = 2 * GROUP
    return pl.pallas_call(
        signal_kernel,
        in_specs=[NEAR, FAR] + [NEAR] * len(ops),
        out_specs=[FAR, FAR, NEAR],
        out_shape=[pltpu.HBM((SIDE, 2 * channels, SIDE), BF16),
                   pltpu.HBM(spec.shape, BF16),
                   jax.ShapeDtypeStruct((groups, GROUP, SIDE), F32)],
        scratch_shapes=[pltpu.VMEM(spec.shape, F32)] + [pltpu.VMEM((rows // OCTET, SIDE * OCTET, SIDE), F32)] * 2 + [held(2 * GROUP)] * 3
        + [pltpu.VMEM(spec.shape, BF16), pltpu.VMEM((groups, SIDE, rows, SIDE), BF16)]
        + [pltpu.SemaphoreType.DMA((groups,))] * 3,
        compiler_params=granted(48),
        cost_estimate=cost(channels * 17 * SIDE, 12 * channels * SIDE * SIDE),
        name="convolve",
    )(got, spec, *ops)


def filter_gradient(cross, tab, scale):
    groups = cross.shape[0]
    channels = groups * GROUP
    ops = [tab[k] for k in ("turn_re", "turn_im", "gather_hi", "gather_lo", "unfold_hi", "unfold_lo")]
    return pl.pallas_call(
        functools.partial(grad_kernel, scale / tab["cross_gain"]),
        grid=(groups,),
        in_specs=[pl.BlockSpec((1, GROUP, SIDE, 2 * SIDE), lambda g: (g, 0, 0, 0))] + [whole(o) for o in ops],
        out_specs=pl.BlockSpec((GROUP, SIDE * SIDE), lambda g: (g, 0)),
        out_shape=jax.ShapeDtypeStruct((channels, SIDE * SIDE), F32),
        scratch_shapes=[pltpu.VMEM((SIDE * GROUP, SIDE), F32), held(GROUP)],
        compiler_params=PARAMS,
        cost_estimate=cost(channels * 5 * SIDE, 12 * channels * SIDE * SIDE),
        name="filter_gradient",
    )(cross, *ops)


PIECES = 4


def chunk(array, i):
    size = array.shape[0] // PIECES
    return array.at[pl.ds(i * size, size)]


def fetches(sources, stores, sems):
    return [[pltpu.make_async_copy(chunk(s, i), chunk(d, i), sems.at[j, i]) for j, (s, d) in enumerate(zip(sources, stores))]
            for i in range(PIECES)]


def products_kernel(query, key_in, value_in, cotangent, out, q, k, v, c, both, in_sem, out_sem):
    loads = fetches((query, key_in, value_in, cotangent), (q, k, v, c), in_sem)
    stores = [s[0] for s in fetches((both,), (out,), out_sem)]
    for group in loads:
        for copy in group:
            copy.start()
    for i in range(PIECES):
        for copy in loads[i]:
            copy.wait()
        qi, ki, vi, ci = [chunk(x, i)[...].astype(F32) for x in (q, k, v, c)]
        pair = jnp.stack([x.reshape(-1, GROUP, SIDE) for x in (ki * vi, ci * qi)], axis=1)
        chunk(both, i)[...] = pair.reshape(chunk(both, i).shape).astype(BF16)
        stores[i].start()
    for copy in stores:
        copy.wait()


def products(query, key_in, value_in, cotangent, own):
    channels = query.shape[0]
    sent = (channels // own, 2 * own, SIDE)
    return pl.pallas_call(
        products_kernel,
        in_specs=[FAR] * 4,
        out_specs=FAR,
        out_shape=jax.ShapeDtypeStruct(sent, BF16),
        scratch_shapes=[pltpu.VMEM(query.shape, BF16)] * 4 + [pltpu.VMEM(sent, BF16)]
        + [pltpu.SemaphoreType.DMA((4, PIECES)), pltpu.SemaphoreType.DMA((1, PIECES))],
        compiler_params=PARAMS,
        cost_estimate=pl.CostEstimate(flops=2 * channels * SIDE, bytes_accessed=12 * channels * SIDE, transcendentals=0),
        name="products",
    )(query, key_in, value_in, cotangent)


def finish_kernel(query, key_in, value_in, cotangent, got, gain, output, grad_query, grad_key, grad_value,
                  k, v, c, spread, out_a, out_b, out_c, out_d, in_sem, out_sem):
    results = (out_a, out_b, out_c, out_d)
    loads = fetches((key_in, value_in, cotangent), (k, v, c), in_sem)
    stores = fetches(results, (output, grad_query, grad_key, grad_value), out_sem)
    for group in loads:
        for j, copy in enumerate(group):
            copy.start(priority=j % 2)
    for i in range(gain.shape[0]):
        spread[i * SIDE:(i + 1) * SIDE, :] = jnp.broadcast_to(gain[i:i + 1, :], (SIDE, SIDE)).T
    for i in range(PIECES):
        for copy in loads[i]:
            copy.wait()
        qi, ki, vi, ci, pair = [chunk(x, i)[...].astype(F32) for x in (query, k, v, c, got)]
        pair = pair.reshape(-1, 2, GROUP, SIDE)
        conv, back = pair[:, 0].reshape(qi.shape), pair[:, 1].reshape(qi.shape)
        g = chunk(spread, i)[...]
        inner = conv + g * (ki * vi).astype(BF16).astype(F32)
        dmixed = back + g * (ci * qi).astype(BF16).astype(F32)
        for store, value in zip(results, (qi * inner, ci * inner, dmixed * vi, dmixed * ki)):
            chunk(store, i)[...] = value.astype(BF16)
        for j, copy in enumerate(stores[i]):
            copy.start(priority=j % 2)
    for group in stores:
        for copy in group:
            copy.wait()


def finish(query, key_in, value_in, cotangent, got, gain):
    channels = query.shape[0]
    return pl.pallas_call(
        finish_kernel,
        in_specs=[NEAR] + [FAR] * 3 + [NEAR] * 2,
        out_specs=[FAR] * 4,
        out_shape=[jax.ShapeDtypeStruct(query.shape, BF16)] * 4,
        scratch_shapes=[pltpu.VMEM(query.shape, BF16)] * 3 + [pltpu.VMEM(query.shape, F32)]
        + [pltpu.VMEM(query.shape, BF16)] * 4
        + [pltpu.SemaphoreType.DMA((3, PIECES)), pltpu.SemaphoreType.DMA((4, PIECES))],
        compiler_params=granted(48),
        cost_estimate=pl.CostEstimate(flops=10 * channels * SIDE, bytes_accessed=20 * channels * SIDE, transcendentals=0),
        name="finish",
    )(query, key_in, value_in, cotangent, got, gain)


def far(array):
    return pltpu.with_memory_space_constraint(array, pltpu.HBM)


def exchange(blocks):
    return lax.all_to_all(blocks, ("node", "local"), split_axis=0, concat_axis=0, tiled=True)


def local(query, key_in, value_in, filters, skip_gain, cotangent):
    tab = tables()
    scale = float(filters.shape[1]) ** -0.5
    got = exchange(products(query, key_in, value_in, cotangent, filters.shape[0]))
    spec = filter_spectra(filters, tab)
    gain = skip_gain.reshape(-1, SIDE)
    send, cross, skip = convolve(got, spec, tab, (1, 1, 2))
    back = exchange(send)
    grad_filters = filter_gradient(cross, tab, scale)
    grad_skip = jnp.sum(skip.reshape(-1, SIDE), axis=1) * scale
    return (*finish(query, far(key_in), far(value_in), far(cotangent), back, gain), grad_filters, grad_skip)


def solution(mesh):
    tokens = P(None, ("node", "local"))
    return jax.shard_map(
        local,
        mesh=mesh,
        in_specs=(tokens, tokens, tokens, P(("node", "local"), None), P(), tokens),
        out_specs=(tokens, tokens, tokens, tokens, P(("node", "local"), None), P(("node", "local"))),
        check_vma=False,
    )
```
